128 devices in a mesh: dp: 16 (over x, z_lo, core), ctx: 8 (over y, z_hi).
Axes of the slice: x: 4, y: 4, z: 4 (z_hi: 2, z_lo: 2; z = z_hi * 2 + z_lo), core: 2. Of those that a mesh axis runs over, the one named last changes fastest.
Arguments:
- hidden: bfloat16 [16, 1024, 5120], P('dp', 'ctx'), may hold values from -6 to 6
- queries: bfloat16 [16, 1024, 8192], P('dp', 'ctx'), may hold values from -6 to 6
- attn_keys: bfloat16 [16, 1024, 1024], P('dp', 'ctx'), may hold values from -6 to 6
- attn_values: bfloat16 [16, 1024, 1024], P('dp', 'ctx'), may hold values from -6 to 6
- attn_output: bfloat16 [16, 1024, 8192], P('dp', 'ctx'), may hold values from -6 to 6
- output_grad: bfloat16 [16, 1024, 8192], P('dp', 'ctx'), may hold values from -6 to 6
- softmax_lse: float32 [16, 64, 1024], P('dp', None, 'ctx'), may hold values from 4 to 7
- doc_lengths: int32 [16, 8], P('dp'), may hold values from 1 to 512, 1024 in all within a row
- stretch_order: int32 [16, 16], P('dp'), may hold values from 0 to 15, each once within a row
Outputs:
- query_grad: bfloat16 [16, 1024, 8192], P('dp', 'ctx')
- key_grad: bfloat16 [16, 1024, 1024], P('dp', 'ctx')
- value_grad: bfloat16 [16, 1024, 1024], P('dp', 'ctx')
- value_weight_grad: float32 [5120, 1024], P(('dp', 'ctx'))
The draws below stay inside these ranges and needn't reach their ends.
Inputs may be any that keep to these rules, and one draw needn't show every extreme that they name: `doc_lengths`: each row holds the lengths of the 8 documents of one sequence in order of position; they sum to 1024 and the longest is exactly 512. Each row names every block of 64 positions of its sequence once: stored block j holds positions stretch_order[b, j] * 64 to stretch_order[b, j] * 64 + 63.
All inputs are finite; a program needn't handle non-finite values.
Results may differ from the reference program's by a relative error of at most 0.0052.
Values may be sent and summed in bfloat16 or wider, within the bound.
A program may use at most 128 MiB of HBM per device.

```python
import math
import jax
import jax.numpy as jnp
import numpy as np
from jax import lax

D = 5120
QH = 64
KVH = 8
HD = 128
NDOC = 8
BATCH = 16
SEQ = 1024
STRETCH = 64
SLOTS = 16


def raised(result, key, source, target, shards_of, factor):
    def block_of(axis_at):
        return (jnp.arange(result.shape[axis_at]) // (result.shape[axis_at] // shards_of)).reshape((-1,) + (1,) * (result.ndim - 1 - axis_at))

    one_side = jax.random.permutation(key, shards_of)[block_of(target)]
    second = (block_of(target) + shards_of // 2) % shards_of
    return jnp.where((block_of(source) == one_side) | (block_of(source) == second), factor * result, result)


def block_scale(key, extent, shards, least, top_value):
    gain = 1.0
    for position, shards_of in shards:
        steps = jax.random.uniform(jax.random.fold_in(jax.random.fold_in(key, 6), position), (shards_of,), jnp.float32, least / len(shards), top_value / len(shards))
        gain = gain * jnp.repeat(jnp.exp(steps), extent[position] // shards_of).reshape((-1,) + (1,) * (len(extent) - 1 - position))
    return gain


def profile(amount, total, limit, lean):
    weights = [(1 << 20) // math.isqrt(rank ** lean) + 1 for rank in range(2, amount + 1)]
    spare, given = total - limit - (amount - 1), [1] * (amount - 1)
    while spare > 0:
        free = [i for i in range(amount - 1) if given[i] < limit]
        whole, budget = sum([weights[i] for i in free]), spare
        for i in free:
            more = min(limit - given[i], max(1, budget * weights[i] // whole), spare)
            given[i] = given[i] + more
            spare = spare - more
    return np.array([limit] + given)


def uneven_parts(key, number_of, total, limit, lean):
    if number_of == 2:
        one = jax.random.randint(key, (), max(1, total - limit), min(limit, total - 1) + 1)
        return jnp.stack([one, total - one])
    tallies = jnp.asarray(profile(number_of, total, limit, lean), jnp.int32)
    couples = (number_of - 1) // 2
    donor, sink = tallies[1:1 + 2 * couples:2], tallies[2:2 + 2 * couples:2]
    slack = jnp.minimum(donor - 1, limit - sink)
    moved = jax.random.randint(jax.random.fold_in(key, 1), (couples,), 0, 1 << 20) % (slack + 1)
    tallies = tallies.at[1:1 + 2 * couples:2].set(donor - moved).at[2:2 + 2 * couples:2].set(sink + moved)
    return tallies[jax.random.permutation(jax.random.fold_in(key, 2), number_of)]


def normal_values(stream_key, shape, scale, reach, cuts=(), kind=jnp.bfloat16):
    factor_of = block_scale(stream_key, shape, cuts, -0.22, 0.18) if cuts else 1.0
    drawn = jax.random.normal(stream_key, shape, jnp.float32) * scale * factor_of
    return jnp.minimum(jnp.maximum(drawn, -reach), reach).astype(kind)


def gaussian_with(rng, dims, width, most, pieces, heavy, kind=jnp.bfloat16):
    drawn = width * jax.random.normal(rng, dims, jnp.float32)
    if pieces:
        drawn = drawn * block_scale(rng, dims, pieces, -0.22, 0.18)
    return jnp.clip(raised(drawn, jax.random.fold_in(rng, 3), *heavy), -most, most).astype(kind)


def setup_inputs(seed: int = 0) -> dict:
    key_of = jax.random.split(jax.random.key(seed), 10)
    hidden = gaussian_with(key_of[0], (BATCH, SEQ, D), 1.0, 6.0, ((0, 16), (1, 8)), (1, 2, 8, 2.0))
    queries = normal_values(key_of[1], (BATCH, SEQ, QH * HD), 1.0, 6.0, ((0, 16), (1, 8)))
    attn_keys = normal_values(key_of[2], (BATCH, SEQ, KVH * HD), 1.0, 6.0, ((0, 16), (1, 8)))
    attn_values = normal_values(key_of[3], (BATCH, SEQ, KVH * HD), 1.0, 6.0, ((0, 16), (1, 8)))
    attn_output = normal_values(key_of[4], (BATCH, SEQ, QH * HD), 1.0, 6.0, ((0, 16), (1, 8)))
    output_grad = normal_values(key_of[5], (BATCH, SEQ, QH * HD), 1.0, 6.0, ((0, 16), (1, 8)))
    softmax_lse = jnp.clip(4.0 + 3.0 * jax.random.uniform(key_of[6], (BATCH, QH, SEQ), jnp.float32) ** block_scale(key_of[6], (BATCH, QH, SEQ), ((0, 16), (2, 8)), -0.2, 0.2), 4.0, 7.0)
    doc_lengths = jax.vmap(lambda own: uneven_parts(own, NDOC, SEQ, SEQ // 2, 2))(jax.random.split(key_of[7], BATCH)).reshape((BATCH, NDOC)).astype(jnp.int32)
    stretch_order = jax.vmap(lambda own: jax.random.permutation(own, SLOTS))(jax.random.split(key_of[8], BATCH)).reshape((BATCH, SLOTS)).astype(jnp.int32)
    return {"hidden": hidden, "queries": queries, "attn_keys": attn_keys, "attn_values": attn_values, "attn_output": attn_output, "output_grad": output_grad, "softmax_lse": softmax_lse, "doc_lengths": doc_lengths, "stretch_order": stretch_order}


def stored_positions(block_order, total_rows, block_len):
    row_ids = jnp.arange(total_rows, dtype=jnp.int32)
    return block_order[row_ids // block_len] * block_len + row_ids % block_len


def document_ids(positions, doc_ends):
    return jnp.sum((positions[:, None] >= doc_ends[None, :]).astype(jnp.int32), axis=1)


def rounded(values):
    return lax.optimization_barrier(values.astype(jnp.bfloat16)).astype(jnp.float32)


def reference(hidden, queries, attn_keys, attn_values, attn_output, output_grad, softmax_lse, doc_lengths, stretch_order):
    head_groups = QH // KVH
    softmax_scale = HD ** -0.5

    def one_pack(pack_index):
        positions = stored_positions(stretch_order[pack_index], SEQ, STRETCH)
        doc_ends = jnp.cumsum(doc_lengths[pack_index], dtype=jnp.int32)
        doc_ids = document_ids(positions, doc_ends)
        allowed = (positions[:, None] >= positions[None, :]) & (doc_ids[:, None] == doc_ids[None, :])
        query_all = queries[pack_index].reshape(SEQ, KVH, head_groups, HD).astype(jnp.float32)
        grad_all = output_grad[pack_index].reshape(SEQ, KVH, head_groups, HD).astype(jnp.float32)
        out_all = attn_output[pack_index].reshape(SEQ, KVH, head_groups, HD).astype(jnp.float32)
        key_all = attn_keys[pack_index].reshape(SEQ, KVH, HD).astype(jnp.float32)
        value_all = attn_values[pack_index].reshape(SEQ, KVH, HD).astype(jnp.float32)
        lse_all = softmax_lse[pack_index].reshape(KVH, head_groups, SEQ)

        def one_group(group_index):
            query_part = query_all[:, group_index]
            grad_part = grad_all[:, group_index]
            out_part = out_all[:, group_index]
            key_part = key_all[:, group_index]
            value_part = value_all[:, group_index]
            lse_part = lse_all[group_index]
            scores = jnp.einsum("sgd,nd->gsn", query_part, key_part) * softmax_scale
            probs = jnp.where(allowed, jnp.exp(scores - lse_part[:, :, None]), 0.0)
            delta = jnp.transpose(jnp.sum(grad_part * out_part, axis=2), (1, 0))
            value_part_grad = jnp.einsum("gsn,sgd->nd", rounded(probs), grad_part)
            prob_grad = jnp.einsum("sgd,nd->gsn", grad_part, value_part)
            score_grad = rounded(probs * (prob_grad - delta[:, :, None]) * softmax_scale)
            query_part_grad = jnp.einsum("gsn,nd->sgd", score_grad, key_part)
            key_part_grad = jnp.einsum("gsn,sgd->nd", score_grad, query_part)
            return query_part_grad, key_part_grad, value_part_grad

        query_stack, key_stack, value_stack = lax.map(one_group, jnp.arange(KVH))
        query_grad = jnp.transpose(query_stack, (1, 0, 2, 3)).reshape(SEQ, QH * HD).astype(jnp.bfloat16)
        key_grad = jnp.transpose(key_stack, (1, 0, 2)).reshape(SEQ, KVH * HD).astype(jnp.bfloat16)
        value_grad = jnp.transpose(value_stack, (1, 0, 2)).reshape(SEQ, KVH * HD).astype(jnp.bfloat16)
        weight_part = jnp.dot(hidden[pack_index].T, value_grad, preferred_element_type=jnp.float32)
        return query_grad, key_grad, value_grad, weight_part

    query_grad, key_grad, value_grad, weight_parts = lax.map(one_pack, jnp.arange(BATCH))
    return query_grad, key_grad, value_grad, jnp.sum(weight_parts, axis=0)
```

```python
import functools
import math

import jax
import jax.numpy as jnp
from jax import lax
from jax.experimental import pallas as pl
from jax.experimental.pallas import tpu as pltpu
from jax.sharding import PartitionSpec as P

MESH = pl.DeviceIdType.MESH
F32 = jnp.float32
BF16 = jnp.bfloat16
KVH = 8
GRP = 8
HD = 128
ROWS = 128
SEQ = 1024
SCALE = HD ** (-0.5)
LOG2E = math.log2(math.e)
BIG = 3.0e38
NB = 256

A0, A1P, A1M, A3P, A3M, B1P, B1M, B2P, B2M, B3 = range(10)


def dot(a, b, ca, cb):
    return lax.dot_general(a, b, (((ca,), (cb,)), ((), ())), preferred_element_type=F32)


def attention_kernel(
    doc_ref, ord_ref, q_ref, k_ref, v_ref, o_ref, do_ref, lse_ref,
    dq_ref, dk_ref, dv_ref,
    kvb, qb, dob, ob, cap, lser, deltar, pf, dqt, dqs,
    s1, r1, s2, r2, s3, r3, fin,
    send, recv, lsem, dqsem,
):
    ctx = lax.axis_index("ctx")
    y, zh = ctx // 2, lax.rem(ctx, 2)
    partner = y * 2 + 1 - zh
    yp, ym, yo = lax.rem(y + 1, 4), lax.rem(y + 3, 4), lax.rem(y + 2, 4)
    up, down = yp * 2 + zh, ym * 2 + zh

    def load_kv(g):
        cols = pl.ds(pl.multiple_of(g * HD, HD), HD)
        rows = pl.ds(pl.multiple_of(ctx * ROWS, ROWS), ROWS)
        pltpu.make_async_copy(k_ref.at[0, :, cols], kvb.at[g, 0, rows], lsem.at[0]).start()
        pltpu.make_async_copy(v_ref.at[0, :, cols], kvb.at[g, 1, rows], lsem.at[0]).start()

    lax.fori_loop(0, KVH, lambda g, c: (load_kv(g), c)[1], 0)

    def load_heads(h, c):
        cols = pl.ds(pl.multiple_of(h * HD, HD), HD)
        g = h // GRP
        rows = pl.ds(pl.multiple_of(lax.rem(h, GRP) * ROWS, ROWS), ROWS)
        pltpu.make_async_copy(do_ref.at[0, :, cols], dob.at[g, rows], lsem.at[1]).start()
        pltpu.make_async_copy(o_ref.at[0, :, cols], ob.at[g, rows], lsem.at[2]).start()
        pltpu.make_async_copy(q_ref.at[0, :, cols], qb.at[g, rows], lsem.at[3]).start()
        return c

    lax.fori_loop(0, KVH * GRP, load_heads, 0)

    barrier = pltpu.get_barrier_semaphore()
    for c in (partner, up, down):
        pl.semaphore_signal(barrier, inc=1, device_id={"ctx": c}, device_id_type=MESH)
    own = pl.ds(pl.multiple_of(ctx * ROWS, ROWS), ROWS)
    pltpu.make_async_copy(kvb.at[:, :, own], kvb.at[:, :, own], lsem.at[0]).wait()
    pl.semaphore_wait(barrier, 3)

    def slot(s):
        return pl.ds(pl.multiple_of(s * 2 * ROWS, 2 * ROWS), 2 * ROWS)

    def half(s, z):
        return pl.ds(pl.multiple_of(s * 2 * ROWS + z * ROWS, ROWS), ROWS)

    def msg(kind, g):
        if kind == A0:
            ref, dst, to = kvb.at[g, :, own], kvb.at[g, :, own], partner
        elif kind == A1P:
            ref, dst, to = kvb.at[g, :, slot(y)], kvb.at[g, :, slot(y)], up
        elif kind == A1M:
            ref, dst, to = kvb.at[g, :, slot(y)], kvb.at[g, :, slot(y)], down
        elif kind == A3P:
            ref, dst, to = kvb.at[g, :, half(ym, 0)], kvb.at[g, :, half(ym, 0)], up
        elif kind == A3M:
            ref, dst, to = kvb.at[g, :, half(yp, 1)], kvb.at[g, :, half(yp, 1)], down
        elif kind == B1P:
            ref, dst, to = s1.at[g, 0], r1.at[g, 0], up
        elif kind == B1M:
            ref, dst, to = s1.at[g, 1], r1.at[g, 1], down
        elif kind == B2P:
            ref, dst, to = s2.at[g, 0], r2.at[g, 0], up
        elif kind == B2M:
            ref, dst, to = s2.at[g, 1], r2.at[g, 1], down
        else:
            ref, dst, to = s3.at[g], r3.at[g], partner
        return pltpu.make_async_remote_copy(
            src_ref=ref, dst_ref=dst, send_sem=send.at[kind, g], recv_sem=recv.at[kind, g],
            device_id={"ctx": to}, device_id_type=MESH,
        )

    def start_a0(g, c):
        msg(A0, g).start()
        return c

    lax.fori_loop(0, KVH, start_a0, 0)

    lane = lax.broadcasted_iota(jnp.int32, (1, ROWS), 1)
    pos_q = jnp.where(
        lane < 64, ord_ref[0, 2 * ctx] * 64 + lane, ord_ref[0, 2 * ctx + 1] * 64 + lane - 64
    )
    start_q = jnp.zeros((1, ROWS), jnp.int32)
    end = jnp.int32(0)
    for j in range(8):
        end = end + doc_ref[0, j]
        start_q = jnp.where(pos_q >= end, end, start_q)
    for j in range(16):
        pos_n = ord_ref[0, j] * 64 + lax.broadcasted_iota(jnp.int32, (64, ROWS), 0)
        seen = (pos_n <= pos_q) & (pos_n >= start_q)
        cap[j * 64:(j + 1) * 64, :] = jnp.where(seen, BIG, -BIG)

    def a1(g):
        msg(A0, g).wait_recv()
        msg(A1P, g).start()
        msg(A1M, g).start()

    def a3(g):
        msg(A1P, g).wait_recv()
        msg(A3P, g).start()
        msg(A1M, g).wait_recv()
        msg(A3M, g).start()

    a1(0)
    a1(1)
    for n in (1, 2, 3):
        ref = (dob, ob, qb)[n - 1]
        pltpu.make_async_copy(ref, ref, lsem.at[n]).wait()

    def rows_of(g, c):
        heads = lse_ref[0, pl.ds(pl.multiple_of(g * GRP, GRP), GRP), :] * LOG2E
        for h in range(GRP):
            cols = slice(h * ROWS, (h + 1) * ROWS)
            prod = dob[g, cols, :].astype(F32) * ob[g, cols, :].astype(F32)
            deltar[g, :, cols] = jnp.sum(prod.T, axis=0, keepdims=True)
            lser[g, :, cols] = heads[h:h + 1, :]
        return c

    lax.fori_loop(0, KVH, rows_of, 0)
    a3(0)

    def compute(g):
        dqt[...] = jnp.zeros_like(dqt)

        def keys(nb, c):
            r = pl.ds(pl.multiple_of(nb * NB, NB), NB)
            kk, vv = kvb[g, 0, r, :], kvb[g, 1, r, :]
            top = cap[r, :]
            top = jnp.concatenate([top, top], axis=1)
            dk = dv = None
            for hp in range(4):
                cols = slice(hp * 256, (hp + 1) * 256)
                qq, dd = qb[g, cols, :], dob[g, cols, :]
                st = dot(kk, qq, 1, 1)
                p = jnp.exp2(jnp.minimum(st * (SCALE * LOG2E) - lser[g, :, cols], top))
                dp = dot(vv, dd, 1, 1)
                ds = (p * (dp - deltar[g, :, cols]) * SCALE).astype(BF16)
                pv, pk = dot(p.astype(BF16), dd, 1, 0), dot(ds, qq, 1, 0)
                dv, dk = (pv, pk) if dv is None else (dv + pv, dk + pk)
                dqt[:, cols] += dot(kk, ds, 0, 0)
            pf[g, 0, r, :] = dk
            pf[g, 1, r, :] = dv
            return c

        lax.fori_loop(0, SEQ // NB, keys, 0)
        for h in range(GRP):
            cols = slice(h * ROWS, (h + 1) * ROWS)
            dqs[g, :, cols] = dqt[:, cols].T.astype(BF16)
        dq_copy(g).start()

    def dq_copy(g):
        cols = pl.ds(pl.multiple_of(g * GRP * HD, GRP * HD), GRP * HD)
        return pltpu.make_async_copy(dqs.at[g], dq_ref.at[0, :, cols], dqsem.at[g])

    def b1(g):
        s1[g, 0] = pf[g, :, half(yo, 0), :].astype(BF16)
        msg(B1P, g).start()
        s1[g, 1] = pf[g, :, half(yo, 1), :].astype(BF16)
        msg(B1M, g).start()

    def b2(g):
        s2[g, 0, :, ROWS:, :] = pf[g, :, half(yp, 1), :].astype(BF16)
        s2[g, 1, :, :ROWS, :] = pf[g, :, half(ym, 0), :].astype(BF16)
        msg(B1P, g).wait_recv()
        s2[g, 0, :, :ROWS, :] = (pf[g, :, half(yp, 0), :] + r1[g, 0].astype(F32)).astype(BF16)
        msg(B2P, g).start()
        msg(B1M, g).wait_recv()
        s2[g, 1, :, ROWS:, :] = (pf[g, :, half(ym, 1), :] + r1[g, 1].astype(F32)).astype(BF16)
        msg(B2M, g).start()

    def b3(g):
        msg(B2P, g).wait_recv()
        msg(B2M, g).wait_recv()

        def total(z):
            rows = pl.ds(pl.multiple_of(z * ROWS, ROWS), ROWS)
            return (
                pf[g, :, half(y, z), :] + r2[g, 0, :, rows, :].astype(F32) + r2[g, 1, :, rows, :].astype(F32)
            )

        s3[g] = total(1 - zh)
        msg(B3, g).start()
        fin[g] = total(zh)

    def b4(g):
        msg(B3, g).wait_recv()
        cols = pl.ds(pl.multiple_of(g * HD, HD), HD)
        done = (fin[g] + r3[g]).astype(BF16)
        dk_ref[0, :, cols] = done[0]
        dv_ref[0, :, cols] = done[1]

    def step(i, c):
        @pl.when(i + 2 < KVH)
        def _():
            a1(i + 2)

        @pl.when(i + 1 < KVH)
        def _():
            a3(i + 1)

        @pl.when(i < KVH)
        def _():
            msg(A3P, i).wait_recv()
            msg(A3M, i).wait_recv()
            compute(i)
            b1(i)

        @pl.when((i >= 1) & (i - 1 < KVH))
        def _():
            b2(i - 1)

        @pl.when((i >= 2) & (i - 2 < KVH))
        def _():
            b3(i - 2)

        @pl.when(i >= 3)
        def _():
            b4(i - 3)

        return c

    lax.fori_loop(0, KVH + 3, step, 0)

    def finish(g, c):
        for kind in range(10):
            msg(kind, g).wait_send()
        dq_copy(g).wait()
        return c

    lax.fori_loop(0, KVH, finish, 0)


def weight_kernel(
    h_ref, vg_ref, out_ref, hid, ht, hg, vgb, dws, dwr, lsem, hs, hr, vs, vr, ws, wr
):
    dp, ctx = lax.axis_index("dp"), lax.axis_index("ctx")
    x, zl, core = dp // 4, lax.rem(dp // 2, 2), lax.rem(dp, 2)
    y, zh = ctx // 2, lax.rem(ctx, 2)
    me = x * 2 + core
    mine = zl * 8 + ctx

    def near(k):
        xx, cc = lax.rem(x + k // 2, 4), lax.rem(core + k % 2, 2)
        return xx, cc, {"dp": (xx * 2 + zl) * 2 + cc}

    def far(k):
        zz = lax.rem(zl + k // 8, 2)
        yy = lax.rem(y + (k // 2) % 4, 4)
        hh = lax.rem(zh + k % 2, 2)
        cc = yy * 2 + hh
        return zz * 8 + cc, {"dp": (x * 2 + zz) * 2 + core, "ctx": cc}

    rows = pl.ds(pl.multiple_of(me * ROWS, ROWS), ROWS)
    load_v = pltpu.make_async_copy(vg_ref.at[0], vgb.at[rows], lsem.at[0])
    load_h = pltpu.make_async_copy(h_ref.at[0], hid, lsem.at[1])
    load_v.start()
    load_h.start()
    barrier = pltpu.get_barrier_semaphore()
    for k in range(1, 8):
        pl.semaphore_signal(barrier, inc=1, device_id=near(k)[2], device_id_type=MESH)
    for k in range(1, 16):
        pl.semaphore_signal(barrier, inc=1, device_id=far(k)[1], device_id_type=MESH)
    load_v.wait()
    pl.semaphore_wait(barrier, 22)

    def send_v(k):
        return pltpu.make_async_remote_copy(
            src_ref=vgb.at[rows], dst_ref=vgb.at[rows], send_sem=vs.at[k], recv_sem=vr.at[k],
            device_id=near(k)[2], device_id_type=MESH,
        )

    def send_h(k, z):
        xx, cc, to = near(k)
        block = (xx * 2 + z) * 2 + cc
        return pltpu.make_async_remote_copy(
            src_ref=ht.at[pl.ds(pl.multiple_of(block * 320, 320), 320)],
            dst_ref=hg.at[z, :, rows],
            send_sem=hs.at[k, z], recv_sem=hr.at[k, z], device_id=to, device_id_type=MESH,
        )

    for k in range(1, 8):
        send_v(k).start()
    load_h.wait()
    for j in range(40):
        ht[j * 128:(j + 1) * 128, :] = hid[:, j * 128:(j + 1) * 128].T
    for k in range(1, 8):
        for z in range(2):
            send_h(k, z).start()
    for z in range(2):
        block = (x * 2 + z) * 2 + core
        hg[z, :, rows] = ht[pl.ds(pl.multiple_of(block * 320, 320), 320), :]

    def send_w(k, p):
        t, to = far(k)
        part = pl.ds(p * 80, 80)
        return pltpu.make_async_remote_copy(
            src_ref=dws.at[t, part], dst_ref=dwr.at[k, part], send_sem=ws.at[p, k], recv_sem=wr.at[p, k],
            device_id=to, device_id_type=MESH,
        )

    for k in range(1, 8):
        send_v(k).wait_recv()
        for z in range(2):
            send_h(k, z).wait_recv()
    for p in range(4):
        res = dot(hg[...].reshape(640, SEQ), vgb[:, p * 256:(p + 1) * 256], 1, 0)
        res = res.reshape(16, 40, 256)
        res = jnp.concatenate([res[:, :, :128], res[:, :, 128:]], axis=1)
        dws[:, p * 80:(p + 1) * 80, :] = res.astype(BF16)
        for k in range(1, 16):
            send_w(k, p).start()
    for p in range(4):
        part = slice(p * 80, (p + 1) * 80)
        acc = dws[mine, part, :].astype(F32)
        for k in range(1, 16):
            send_w(k, p).wait_recv()
            acc = acc + dwr[k, part, :].astype(F32)
        out_ref[:, p * 256:p * 256 + 128] = acc[:40]
        out_ref[:, p * 256 + 128:(p + 1) * 256] = acc[40:]
    for k in range(1, 8):
        send_v(k).wait_send()
        for z in range(2):
            send_h(k, z).wait_send()
    for p in range(4):
        for k in range(1, 16):
            send_w(k, p).wait_send()


def body(hidden, q, k, v, o, do, lse, docs, order):
    anyspace = pl.BlockSpec(memory_space=pl.ANY)
    vmem = pl.BlockSpec(memory_space=pltpu.VMEM)
    smem = pl.BlockSpec(memory_space=pltpu.SMEM)
    dma = pltpu.SemaphoreType.DMA
    dq, dk, dv = pl.pallas_call(
        attention_kernel,
        out_shape=(
            jax.ShapeDtypeStruct((1, ROWS, KVH * GRP * HD), BF16),
            jax.ShapeDtypeStruct((1, ROWS, KVH * HD), BF16),
            jax.ShapeDtypeStruct((1, ROWS, KVH * HD), BF16),
        ),
        in_specs=[smem, smem, anyspace, anyspace, anyspace, anyspace, anyspace, vmem],
        out_specs=(anyspace, vmem, vmem),
        scratch_shapes=[
            pltpu.VMEM((KVH, 2, SEQ, HD), BF16),
            pltpu.VMEM((KVH, GRP * ROWS, HD), BF16),
            pltpu.VMEM((KVH, GRP * ROWS, HD), BF16),
            pltpu.VMEM((KVH, GRP * ROWS, HD), BF16),
            pltpu.VMEM((SEQ, ROWS), F32),
            pltpu.VMEM((KVH, 1, GRP * ROWS), F32),
            pltpu.VMEM((KVH, 1, GRP * ROWS), F32),
            pltpu.VMEM((KVH, 2, SEQ, HD), F32),
            pltpu.VMEM((HD, GRP * ROWS), F32),
            pltpu.VMEM((KVH, ROWS, GRP * HD), BF16),
            pltpu.VMEM((KVH, 2, 2, ROWS, HD), BF16),
            pltpu.VMEM((KVH, 2, 2, ROWS, HD), BF16),
            pltpu.VMEM((KVH, 2, 2, 2 * ROWS, HD), BF16),
            pltpu.VMEM((KVH, 2, 2, 2 * ROWS, HD), BF16),
            pltpu.VMEM((KVH, 2, ROWS, HD), F32),
            pltpu.VMEM((KVH, 2, ROWS, HD), F32),
            pltpu.VMEM((KVH, 2, ROWS, HD), F32),
            dma((10, KVH)), dma((10, KVH)), dma((4,)), dma((KVH,)),
        ],
        compiler_params=pltpu.CompilerParams(
            collective_id=0, has_side_effects=True, vmem_limit_bytes=56 * 2**20
        ),
        name="attention",
    )(docs, order, q, k, v, o, do, lse)
    dw = pl.pallas_call(
        weight_kernel,
        out_shape=jax.ShapeDtypeStruct((40, KVH * HD), F32),
        in_specs=[anyspace, anyspace],
        out_specs=vmem,
        scratch_shapes=[
            pltpu.VMEM((ROWS, 5120), BF16),
            pltpu.VMEM((5120, ROWS), BF16),
            pltpu.VMEM((2, 320, SEQ), BF16),
            pltpu.VMEM((SEQ, KVH * HD), BF16),
            pltpu.VMEM((16, 320, 128), BF16),
            pltpu.VMEM((16, 320, 128), BF16),
            dma((2,)), dma((8, 2)), dma((8, 2)), dma((8,)), dma((8,)), dma((4, 16)), dma((4, 16)),
        ],
        compiler_params=pltpu.CompilerParams(
            collective_id=1, has_side_effects=True, vmem_limit_bytes=48 * 2**20
        ),
        name="weights",
    )(hidden, dv)
    return dq, dk, dv, dw


def solution(mesh):
    placed = (P("dp", "ctx", None),) * 6 + (P("dp", None, "ctx"), P("dp", None), P("dp", None))
    return jax.shard_map(
        body,
        mesh=mesh,
        in_specs=placed,
        out_specs=(P("dp", "ctx", None),) * 3 + (P(("dp", "ctx"), None),),
        check_vma=False,
    )
```

```python
import math

import jax
import jax.numpy as jnp
from jax import lax
from jax.experimental import pallas as pl
from jax.experimental.pallas import tpu as pltpu
from jax.sharding import PartitionSpec as P

MESH = pl.DeviceIdType.MESH
F32 = jnp.float32
BF16 = jnp.bfloat16
KVH = 8
GRP = 8
HD = 128
ROWS = 128
SEQ = 1024
SCALE = HD ** (-0.5)
LOG2E = math.log2(math.e)
BIG = 3.0e38
NB = 256

A0, A1P, A1M, A3P, A3M = range(5)
V1P, V1M, V2P, V2M, Z0, ZP, ZM, ZO = range(5, 13)
B1P, B1M, B2P, B2M, B3 = range(13, 18)
W0, W1P, W1M, W2P, W2M = range(18, 23)
KINDS = 23


def dot(a, b, ca, cb):
    return lax.dot_general(a, b, (((ca,), (cb,)), ((), ())), preferred_element_type=F32)


def rng(start, size):
    return pl.ds(pl.multiple_of(start, size), size)


def kernel(
    doc_ref, ord_ref, q_ref, k_ref, v_ref, o_ref, do_ref, lse_ref, h_ref,
    dq_ref, dk_ref, dv_ref, dw_ref,
    kvb, qb, dob, ob, cap, lser, deltar, pf, dqt, dqs,
    s1, r1, s2, r2, s3, r3, fin, w0s, w0r, w1s, w1r, w2s, w2r,
    hid, ht, hg, vgb, dws, dwr,
    send, recv, lsem, dqsem, hs, hr, vs, vr, ws, wr,
):
    dp, ctx = lax.axis_index("dp"), lax.axis_index("ctx")
    x, zl, core = dp // 4, lax.rem(dp // 2, 2), lax.rem(dp, 2)
    y, zh = ctx // 2, lax.rem(ctx, 2)
    partner = y * 2 + 1 - zh
    yp, ym, yo = lax.rem(y + 1, 4), lax.rem(y + 3, 4), lax.rem(y + 2, 4)
    up, down = yp * 2 + zh, ym * 2 + zh
    me = x * 2 + core
    mine = zl * 8 + ctx

    def load_kv(g, c):
        cols, rows = rng(g * HD, HD), rng(ctx * ROWS, ROWS)
        pltpu.make_async_copy(k_ref.at[0, :, cols], kvb.at[g, 0, rows], lsem.at[0]).start()
        pltpu.make_async_copy(v_ref.at[0, :, cols], kvb.at[g, 1, rows], lsem.at[0]).start()
        return c

    lax.fori_loop(0, KVH, load_kv, 0)

    def load_heads(h, c):
        cols = rng(h * HD, HD)
        g = h // GRP
        rows = rng(lax.rem(h, GRP) * ROWS, ROWS)
        pltpu.make_async_copy(do_ref.at[0, :, cols], dob.at[g, rows], lsem.at[1]).start()
        pltpu.make_async_copy(o_ref.at[0, :, cols], ob.at[g, rows], lsem.at[2]).start()
        pltpu.make_async_copy(q_ref.at[0, :, cols], qb.at[g, rows], lsem.at[3]).start()
        return c

    lax.fori_loop(0, KVH * GRP, load_heads, 0)
    load_hidden = pltpu.make_async_copy(h_ref.at[0], hid, lsem.at[4])
    load_hidden.start()

    def near(k):
        xx, cc = lax.rem(x + k // 2, 4), lax.rem(core + lax.rem(k, 2), 2)
        return xx, cc, {"dp": (xx * 2 + zl) * 2 + cc}

    def far(k):
        zz = lax.rem(zl + k // 8, 2)
        yy = lax.rem(y + lax.rem(k // 2, 4), 4)
        cc = yy * 2 + lax.rem(zh + lax.rem(k, 2), 2)
        return zz * 8 + cc, {"dp": (x * 2 + zz) * 2 + core, "ctx": cc}

    barrier = pltpu.get_barrier_semaphore()
    for k in range(1, 8):
        pl.semaphore_signal(barrier, inc=1, device_id=near(k)[2], device_id_type=MESH)
    for k in range(1, 16):
        pl.semaphore_signal(barrier, inc=1, device_id=far(k)[1], device_id_type=MESH)
    own = rng(ctx * ROWS, ROWS)
    pltpu.make_async_copy(kvb.at[:, :, own], kvb.at[:, :, own], lsem.at[0]).wait()
    pl.semaphore_wait(barrier, 22)

    def slot(s):
        return rng(s * 2 * ROWS, 2 * ROWS)

    def half(s, z):
        return rng((s * 2 + z) * ROWS, ROWS)

    def quarter(s, z, n):
        return rng((s * 4 + z * 2 + n) * 64, 64)

    def msg(kind, g):
        same = {
            A0: (0, own, partner),
            A1P: (0, slot(y), up),
            A1M: (0, slot(y), down),
            A3P: (0, half(ym, 0), up),
            A3M: (0, half(yp, 1), down),
            V1P: (1, own, up),
            V1M: (1, own, down),
            V2P: (1, quarter(ym, zh, 0), up),
            V2M: (1, quarter(yp, zh, 1), down),
            Z0: (1, own, partner),
            ZP: (1, half(yp, zh), partner),
            ZM: (1, half(ym, zh), partner),
            ZO: (1, half(yo, zh), partner),
        }
        other = {
            B1P: (s1.at[g, 0], r1.at[g, 0], up),
            B1M: (s1.at[g, 1], r1.at[g, 1], down),
            B2P: (s2.at[g, 0], r2.at[g, 0], up),
            B2M: (s2.at[g, 1], r2.at[g, 1], down),
            B3: (s3.at[g], r3.at[g], partner),
            W0: (w0s.at[g], w0r.at[g], partner),
            W1P: (w1s.at[g, 0], w1r.at[g, 0], up),
            W1M: (w1s.at[g, 1], w1r.at[g, 1], down),
            W2P: (w2s.at[g, 0], w2r.at[g, 0], up),
            W2M: (w2s.at[g, 1], w2r.at[g, 1], down),
        }
        if kind in same:
            which, rows, to = same[kind]
            src = dst = kvb.at[g, which, rows]
        else:
            src, dst, to = other[kind]
        return pltpu.make_async_remote_copy(
            src_ref=src, dst_ref=dst, send_sem=send.at[kind, g], recv_sem=recv.at[kind, g],
            device_id={"ctx": to}, device_id_type=MESH,
        )

    def go(g, *kinds):
        for kind in kinds:
            msg(kind, g).start()

    def take(g, *kinds):
        for kind in kinds:
            msg(kind, g).wait_recv()

    def gather0(g):
        go(g, A0, V1P, V1M, Z0)

    def gather1(g):
        take(g, A0)
        go(g, A1P, A1M)
        take(g, V1P)
        go(g, V2P, ZM)
        take(g, V1M)
        go(g, V2M, ZP)

    def gather2(g):
        take(g, A1P)
        go(g, A3P)
        take(g, A1M)
        go(g, A3M)
        take(g, V2P, V2M)
        go(g, ZO)

    for g in range(3):
        gather0(g)

    lane = lax.broadcasted_iota(jnp.int32, (1, ROWS), 1)
    pos_q = jnp.where(
        lane < 64, ord_ref[0, 2 * ctx] * 64 + lane, ord_ref[0, 2 * ctx + 1] * 64 + lane - 64
    )
    start_q = jnp.zeros((1, ROWS), jnp.int32)
    end = jnp.int32(0)
    for j in range(8):
        end = end + doc_ref[0, j]
        start_q = jnp.where(pos_q >= end, end, start_q)
    for j in range(16):
        pos_n = ord_ref[0, j] * 64 + lax.broadcasted_iota(jnp.int32, (64, ROWS), 0)
        seen = (pos_n <= pos_q) & (pos_n >= start_q)
        cap[j * 64:(j + 1) * 64, :] = jnp.where(seen, BIG, -BIG)

    gather1(0)
    gather1(1)
    for n in (1, 2, 3):
        ref = (dob, ob, qb)[n - 1]
        pltpu.make_async_copy(ref, ref, lsem.at[n]).wait()
    load_hidden.wait()
    gather2(0)

    def rows_of(g):
        heads = lse_ref[0, rng(g * GRP, GRP), :] * LOG2E
        for h in range(GRP):
            cols = slice(h * ROWS, (h + 1) * ROWS)
            prod = dob[g, cols, :].astype(F32) * ob[g, cols, :].astype(F32)
            deltar[g, :, cols] = jnp.sum(prod.T, axis=0, keepdims=True)
            lser[g, :, cols] = heads[h:h + 1, :]

    def compute(g):
        dqt[...] = jnp.zeros_like(dqt)

        def keys(nb, c):
            r = rng(nb * NB, NB)
            kk, vv = kvb[g, 0, r, :], kvb[g, 1, r, :]
            top = cap[r, :]
            top = jnp.concatenate([top, top], axis=1)
            dk = dv = None
            for hp in range(4):
                cols = slice(hp * 256, (hp + 1) * 256)
                qq, dd = qb[g, cols, :], dob[g, cols, :]
                st = dot(kk, qq, 1, 1)
                p = jnp.exp2(jnp.minimum(st * (SCALE * LOG2E) - lser[g, :, cols], top))
                dp_ = dot(vv, dd, 1, 1)
                ds = (p * (dp_ - deltar[g, :, cols]) * SCALE).astype(BF16)
                pv, pk = dot(p.astype(BF16), dd, 1, 0), dot(ds, qq, 1, 0)
                dv, dk = (pv, pk) if dv is None else (dv + pv, dk + pk)
                dqt[:, cols] += dot(kk, ds, 0, 0)
            pf[g, 0, r, :] = dk
            pf[g, 1, r, :] = dv
            return c

        lax.fori_loop(0, SEQ // NB, keys, 0)
        for h in range(GRP):
            cols = slice(h * ROWS, (h + 1) * ROWS)
            dqs[g, :, cols] = dqt[:, cols].T.astype(BF16)
        dq_copy(g).start()

    def dq_copy(g):
        return pltpu.make_async_copy(dqs.at[g], dq_ref.at[0, :, rng(g * GRP * HD, GRP * HD)], dqsem.at[g])

    def sum1(g):
        s1[g, 0] = pf[g, 0, half(yo, 0), :].astype(BF16)
        s1[g, 1] = pf[g, 0, half(yo, 1), :].astype(BF16)
        go(g, B1P, B1M)
        for s in range(4):
            w0s[g, s] = pf[g, 1, half(s, 1 - zh), :].astype(BF16)
        go(g, W0)

    def sum2(g):
        s2[g, 0, ROWS:, :] = pf[g, 0, half(yp, 1), :].astype(BF16)
        s2[g, 1, :ROWS, :] = pf[g, 0, half(ym, 0), :].astype(BF16)
        take(g, B1P)
        s2[g, 0, :ROWS, :] = (pf[g, 0, half(yp, 0), :] + r1[g, 0].astype(F32)).astype(BF16)
        go(g, B2P)
        take(g, B1M)
        s2[g, 1, ROWS:, :] = (pf[g, 0, half(ym, 1), :] + r1[g, 1].astype(F32)).astype(BF16)
        go(g, B2M)
        take(g, W0)
        for s in range(4):
            pf[g, 1, half(s, zh), :] += w0r[g, s].astype(F32)
        w1s[g, 0] = pf[g, 1, quarter(yo, zh, 0), :].astype(BF16)
        w1s[g, 1] = pf[g, 1, quarter(yo, zh, 1), :].astype(BF16)
        go(g, W1P, W1M)

    def sum3(g):
        w2s[g, 0, 64:, :] = pf[g, 1, quarter(yp, zh, 1), :].astype(BF16)
        w2s[g, 1, :64, :] = pf[g, 1, quarter(ym, zh, 0), :].astype(BF16)
        take(g, W1P)
        w2s[g, 0, :64, :] = (pf[g, 1, quarter(yp, zh, 0), :] + w1r[g, 0].astype(F32)).astype(BF16)
        go(g, W2P)
        take(g, W1M)
        w2s[g, 1, 64:, :] = (pf[g, 1, quarter(ym, zh, 1), :] + w1r[g, 1].astype(F32)).astype(BF16)
        go(g, W2M)
        take(g, B2P, B2M)

        def total(z):
            rows = rng(z * ROWS, ROWS)
            return pf[g, 0, half(y, z), :] + r2[g, 0, rows, :].astype(F32) + r2[g, 1, rows, :].astype(F32)

        s3[g] = total(1 - zh).astype(BF16)
        go(g, B3)
        fin[g] = total(zh)

    def sum4(g):
        cols = rng(g * HD, HD)
        take(g, W2P, W2M)
        dv = (pf[g, 1, own, :] + w2r[g, 0].astype(F32) + w2r[g, 1].astype(F32)).astype(BF16)
        dv_ref[0, :, cols] = dv
        vgb[g // 2, rng(me * ROWS, ROWS), rng(lax.rem(g, 2) * HD, HD)] = dv
        take(g, B3)
        dk_ref[0, :, cols] = (fin[g] + r3[g].astype(F32)).astype(BF16)

    def send_h(k, z):
        xx, cc, to = near(k)
        return pltpu.make_async_remote_copy(
            src_ref=ht.at[rng(((xx * 2 + z) * 2 + cc) * 320, 320)],
            dst_ref=hg.at[z, :, rng(me * ROWS, ROWS)],
            send_sem=hs.at[k, z], recv_sem=hr.at[k, z], device_id=to, device_id_type=MESH,
        )

    def turn(i):
        dx, z = i // 2, lax.rem(i, 2)
        j = lax.rem(x + dx, 4) * 2 + z
        for n in range(5):
            at = j * 640 + n * 128
            ht[rng(at, 128), :] = hid[:, rng(at, 128)].T
        send_h(dx * 2 + 1, z).start()

        @pl.when(dx > 0)
        def _():
            send_h(dx * 2, z).start()

        @pl.when(dx == 0)
        def _():
            hg[z, :, rng(me * ROWS, ROWS)] = ht[rng((j * 2 + core) * 320, 320), :]

    def send_v(k, p):
        rows = rng(me * ROWS, ROWS)
        return pltpu.make_async_remote_copy(
            src_ref=vgb.at[p, rows], dst_ref=vgb.at[p, rows], send_sem=vs.at[p, k], recv_sem=vr.at[p, k],
            device_id=near(k)[2], device_id_type=MESH,
        )

    def send_w(k, p):
        t, to = far(k)
        return pltpu.make_async_remote_copy(
            src_ref=dws.at[p, t], dst_ref=dwr.at[p, k], send_sem=ws.at[p, k], recv_sem=wr.at[p, k],
            device_id=to, device_id_type=MESH,
        )

    def each(lo, hi, f):
        def one(k, c):
            f(k)
            return c

        lax.fori_loop(lo, hi, one, 0)

    def weights1(p):
        each(1, 8, lambda k: send_v(k, p).start())

    def weights2(p):
        @pl.when(p == 0)
        def _():
            def arrived(k):
                send_h(k, 0).wait_recv()
                send_h(k, 1).wait_recv()

            each(1, 8, arrived)

        each(1, 8, lambda k: send_v(k, p).wait_recv())
        res = dot(hg[...].reshape(640, SEQ), vgb[p], 1, 0).reshape(16, 40, 256)
        dws[p] = jnp.concatenate([res[:, :, :128], res[:, :, 128:]], axis=1).astype(BF16)
        each(1, 16, lambda k: send_w(k, p).start())

    def weights3(p):
        each(1, 16, lambda k: send_w(k, p).wait_recv())
        acc = dws[p, mine].astype(F32)
        for k in range(1, 16):
            acc = acc + dwr[p, k].astype(F32)
        dw_ref[:, rng(p * 256, 128)] = acc[:40]
        dw_ref[:, rng(p * 256 + 128, 128)] = acc[40:]

    def at(i, lo, count, f):
        @pl.when((i >= lo) & (i < lo + count))
        def _():
            f(i - lo)

    def at_pair(i, lo, f):
        @pl.when((i >= lo) & (i < lo + 8) & (lax.rem(i - lo, 2) == 0))
        def _():
            f((i - lo) // 2)

    def step(i, c):
        at(i, -3, KVH, gather0)
        at(i, -2, KVH, gather1)
        at(i, -1, KVH, gather2)

        @pl.when(i < KVH)
        def _():
            @pl.when(i < 4)
            def _():
                turn(2 * i)
                turn(2 * i + 1)

            rows_of(i)
            take(i, A3P, A3M, Z0, ZP, ZM, ZO)
            compute(i)
            sum1(i)

        at(i, 1, KVH, sum2)
        at(i, 2, KVH, sum3)
        at(i, 3, KVH, sum4)
        at_pair(i, 4, weights1)
        at_pair(i, 5, weights2)
        at_pair(i, 7, weights3)
        return c

    lax.fori_loop(0, 14, step, 0)

    def finish(g, c):
        for kind in range(KINDS):
            msg(kind, g).wait_send()
        dq_copy(g).wait()
        return c

    lax.fori_loop(0, KVH, finish, 0)

    def sent_near(k):
        for z in range(2):
            send_h(k, z).wait_send()
        for p in range(4):
            send_v(k, p).wait_send()

    def sent_far(k):
        for p in range(4):
            send_w(k, p).wait_send()

    each(1, 8, sent_near)
    each(1, 16, sent_far)


def body(hidden, q, k, v, o, do, lse, docs, order):
    anyspace = pl.BlockSpec(memory_space=pl.ANY)
    vmem = pl.BlockSpec(memory_space=pltpu.VMEM)
    smem = pl.BlockSpec(memory_space=pltpu.SMEM)
    dma = pltpu.SemaphoreType.DMA
    return pl.pallas_call(
        kernel,
        out_shape=(
            jax.ShapeDtypeStruct((1, ROWS, KVH * GRP * HD), BF16),
            jax.ShapeDtypeStruct((1, ROWS, KVH * HD), BF16),
            jax.ShapeDtypeStruct((1, ROWS, KVH * HD), BF16),
            jax.ShapeDtypeStruct((40, KVH * HD), F32),
        ),
        in_specs=[smem, smem] + [anyspace] * 5 + [vmem, anyspace],
        out_specs=(anyspace, vmem, vmem, vmem),
        scratch_shapes=[
            pltpu.VMEM((KVH, 2, SEQ, HD), BF16),
            pltpu.VMEM((KVH, GRP * ROWS, HD), BF16),
            pltpu.VMEM((KVH, GRP * ROWS, HD), BF16),
            pltpu.VMEM((KVH, GRP * ROWS, HD), BF16),
            pltpu.VMEM((SEQ, ROWS), F32),
            pltpu.VMEM((KVH, 1, GRP * ROWS), F32),
            pltpu.VMEM((KVH, 1, GRP * ROWS), F32),
            pltpu.VMEM((KVH, 2, SEQ, HD), F32),
            pltpu.VMEM((HD, GRP * ROWS), F32),
            pltpu.VMEM((KVH, ROWS, GRP * HD), BF16),
            pltpu.VMEM((KVH, 2, ROWS, HD), BF16),
            pltpu.VMEM((KVH, 2, ROWS, HD), BF16),
            pltpu.VMEM((KVH, 2, 2 * ROWS, HD), BF16),
            pltpu.VMEM((KVH, 2, 2 * ROWS, HD), BF16),
            pltpu.VMEM((KVH, ROWS, HD), BF16),
            pltpu.VMEM((KVH, ROWS, HD), BF16),
            pltpu.VMEM((KVH, ROWS, HD), F32),
            pltpu.VMEM((KVH, 4, ROWS, HD), BF16),
            pltpu.VMEM((KVH, 4, ROWS, HD), BF16),
            pltpu.VMEM((KVH, 2, 64, HD), BF16),
            pltpu.VMEM((KVH, 2, 64, HD), BF16),
            pltpu.VMEM((KVH, 2, ROWS, HD), BF16),
            pltpu.VMEM((KVH, 2, ROWS, HD), BF16),
            pltpu.VMEM((ROWS, 5120), BF16),
            pltpu.VMEM((5120, ROWS), BF16),
            pltpu.VMEM((2, 320, SEQ), BF16),
            pltpu.VMEM((4, SEQ, 256), BF16),
            pltpu.VMEM((4, 16, 80, 128), BF16),
            pltpu.VMEM((4, 16, 80, 128), BF16),
            dma((KINDS, KVH)), dma((KINDS, KVH)), dma((5,)), dma((KVH,)),
            dma((8, 2)), dma((8, 2)), dma((4, 8)), dma((4, 8)), dma((4, 16)), dma((4, 16)),
        ],
        compiler_params=pltpu.CompilerParams(
            collective_id=0, has_side_effects=True, vmem_limit_bytes=56 * 2**20
        ),
        name="attention_and_weights",
    )(docs, order, q, k, v, o, do, lse, hidden)


def solution(mesh):
    placed = (P("dp", "ctx", None),) * 6 + (P("dp", None, "ctx"), P("dp", None), P("dp", None))
    return jax.shard_map(
        body,
        mesh=mesh,
        in_specs=placed,
        out_specs=(P("dp", "ctx", None),) * 3 + (P(("dp", "ctx"), None),),
        check_vma=False,
    )
```

```python
import math

import jax
import jax.numpy as jnp
from jax import lax
from jax.experimental import pallas as pl
from jax.experimental.pallas import tpu as pltpu
from jax.sharding import PartitionSpec as P

MESH = pl.DeviceIdType.MESH
F32 = jnp.float32
BF16 = jnp.bfloat16
KVH = 8
GRP = 8
HD = 128
ROWS = 128
SEQ = 1024
SCALE = HD ** (-0.5)
LOG2E = math.log2(math.e)
BIG = 3.0e38
NB = 1024
K1, K2, V0, V1, V2 = -6, -3, 0, 3, 6
D2, D3, D4 = 3, 6, 8
E2, E3, E4 = 11, 14, 17
G1, G2, G3, G4 = 9, 12, 14, 16

A0, A1P, A1M, A3P, A3M = range(5)
V1P, V1M, V2P, V2M, Z0, ZP, ZM, ZO = range(5, 13)
B1P, B1M, B2P, B2M, B3 = range(13, 18)
W0, W1P, W1M, W2P, W2M = range(18, 23)
SEM = (0, 1, 1, 2, 2) + (0, 0, 1, 1, 2, 2, 2, 2) + (3, 3, 4, 4, 5) + (3, 4, 4, 5, 5)
SENT = 896


def dot(a, b, ca, cb):
    return lax.dot_general(a, b, (((ca,), (cb,)), ((), ())), preferred_element_type=F32)


def rng(start, size):
    return pl.ds(pl.multiple_of(start, size), size)


def kernel(
    doc_ref, ord_ref, q_ref, k_ref, v_ref, o_ref, do_ref, lse_ref, h_ref,
    dq_ref, dk_ref, dv_ref, dw_ref,
    kvb, qb, dob, ob, cap, lser, deltar, pf, dqt, probs, lse,
    s1, r1, s2, r2, s3, r3, fin, w0s, w0r, w1s, w1r, w2s, w2r,
    hid, ht, hg, vgb, dws, dwr, dus, dur,
    send, recv, lsem, hsem, dqsem, hs, hr, vs, vr, ws, wr, us, ur,
):
    dp, ctx = lax.axis_index("dp"), lax.axis_index("ctx")
    x, zl, core = dp // 4, lax.rem(dp // 2, 2), lax.rem(dp, 2)
    y, zh = ctx // 2, lax.rem(ctx, 2)
    partner = y * 2 + 1 - zh
    yp, ym, yo = lax.rem(y + 1, 4), lax.rem(y + 3, 4), lax.rem(y + 2, 4)
    up, down = yp * 2 + zh, ym * 2 + zh
    me = x * 2 + core
    mine = zl * 2 + zh

    def near(k):
        xx, cc = lax.rem(x + k // 2, 4), lax.rem(core + lax.rem(k, 2), 2)
        return xx, cc, {"dp": (xx * 2 + zl) * 2 + cc}

    def along_y(k):
        yy = lax.rem(y + k, 4)
        return yy, {"ctx": yy * 2 + zh}

    def along_z(k):
        zz, hh = lax.rem(zl + k // 2, 2), lax.rem(zh + lax.rem(k, 2), 2)
        return zz * 2 + hh, {"dp": (x * 2 + zz) * 2 + core, "ctx": y * 2 + hh}

    barrier = pltpu.get_barrier_semaphore()
    for k in range(1, 8):
        pl.semaphore_signal(barrier, inc=1, device_id=near(k)[2], device_id_type=MESH)
    for k in range(1, 4):
        pl.semaphore_signal(barrier, inc=1, device_id=along_y(k)[1], device_id_type=MESH)
        pl.semaphore_signal(barrier, inc=1, device_id=along_z(k)[1], device_id_type=MESH)
    def load_kv(g, c):
        cols, rows = rng(g * HD, HD), rng(ctx * ROWS, ROWS)
        pltpu.make_async_copy(k_ref.at[0, :, cols], kvb.at[g, 0, rows], lsem.at[0]).start()
        pltpu.make_async_copy(v_ref.at[0, :, cols], kvb.at[g, 1, rows], lsem.at[0]).start()
        return c

    lax.fori_loop(0, KVH, load_kv, 0)

    own = rng(ctx * ROWS, ROWS)
    pltpu.make_async_copy(kvb.at[:, :, own], kvb.at[:, :, own], lsem.at[0]).wait()
    pl.semaphore_wait(barrier, 13)

    def slot(s):
        return rng(s * 2 * ROWS, 2 * ROWS)

    def half(s, z):
        return rng((s * 2 + z) * ROWS, ROWS)

    def quarter(s, z, n):
        return rng((s * 4 + z * 2 + n) * 64, 64)

    def msg(kind, w, g):
        same = {
            A0: (own, partner),
            A1P: (slot(y), up),
            A1M: (slot(y), down),
            A3P: (half(ym, 0), up),
            A3M: (half(yp, 1), down),
            V1P: (own, up),
            V1M: (own, down),
            V2P: (quarter(ym, zh, 0), up),
            V2M: (quarter(yp, zh, 1), down),
            Z0: (own, partner),
            ZP: (half(yp, zh), partner),
            ZM: (half(ym, zh), partner),
            ZO: (half(yo, zh), partner),
        }
        j = w * 4 + g // 2
        other = {
            B1P: (s1.at[j, 0], r1.at[j, 0], up),
            B1M: (s1.at[j, 1], r1.at[j, 1], down),
            B2P: (s2.at[j, 0], r2.at[j, 0], up),
            B2M: (s2.at[j, 1], r2.at[j, 1], down),
            B3: (s3.at[j], r3.at[j], partner),
            W0: (w0s.at[j], w0r.at[j], partner),
            W1P: (w1s.at[j, 0], w1r.at[j, 0], up),
            W1M: (w1s.at[j, 1], w1r.at[j, 1], down),
            W2P: (w2s.at[j, 0], w2r.at[j, 0], up),
            W2M: (w2s.at[j, 1], w2r.at[j, 1], down),
        }
        if kind in same:
            rows, to = same[kind]
            src = dst = kvb.at[g, w, rows]
        else:
            src, dst, to = other[kind]
        return pltpu.make_async_remote_copy(
            src_ref=src, dst_ref=dst, send_sem=send.at[w, kind // 13], recv_sem=recv.at[SEM[kind], w * KVH + g],
            device_id={"ctx": to}, device_id_type=MESH,
        )

    def go(w, g, *kinds):
        for kind in kinds:
            msg(kind, w, g).start()

    def take(w, g, kind, rows):
        whole = kvb.at[g, w, pl.ds(0, rows)]
        pltpu.make_async_copy(whole, whole, recv.at[SEM[kind], w * KVH + g]).wait()

    def wait(ref, sem):
        pltpu.make_async_copy(ref, ref, sem).wait()

    def each(lo, hi, f):
        def one(k, c):
            f(k)
            return c

        lax.fori_loop(lo, hi, one, 0)

    def either(w, first, second):
        def run(g):
            even = lax.rem(g + w, 2) == 0

            @pl.when(even)
            def _():
                first(w, g)

            @pl.when(jnp.logical_not(even))
            def _():
                second(w, g)

        return run

    def zy0(w, g):
        go(w, g, A0)

    def zy1(w, g):
        take(w, g, A0, ROWS)
        go(w, g, A1P, A1M)

    def zy2(w, g):
        take(w, g, A1P, 4 * ROWS)
        go(w, g, A3P, A3M)

    def zy3(w, g):
        take(w, g, A3P, 2 * ROWS)

    def yz0(w, g):
        go(w, g, V1P, V1M, Z0)

    def yz1(w, g):
        take(w, g, V1P, 2 * ROWS)
        go(w, g, V2P, V2M, ZM, ZP)

    def yz2(w, g):
        take(w, g, V2P, ROWS)
        go(w, g, ZO)

    def yz3(w, g):
        take(w, g, Z0, 4 * ROWS)

    keys = [either(0, *two) for two in ((zy0, yz0), (zy1, yz1), (zy2, yz2), (zy3, yz3))]
    values = [either(1, *two) for two in ((zy0, yz0), (zy1, yz1), (zy2, yz2), (zy3, yz3))]

    each(0, KVH, keys[0])

    load_lse = pltpu.make_async_copy(lse_ref.at[0], lse, lsem.at[2])
    load_lse.start()
    load_hidden = pltpu.make_async_copy(h_ref.at[0], hid, lsem.at[1])
    load_hidden.start()

    def load_heads(g):
        cols = rng(g * GRP * HD, GRP * HD)
        return [
            pltpu.make_async_copy(ref.at[0, :, cols], buf.at[g], hsem.at[g])
            for ref, buf in ((do_ref, dob), (o_ref, ob), (q_ref, qb))
        ]

    def start_heads(g, c):
        for copy in load_heads(g):
            copy.start()
        return c

    lax.fori_loop(0, KVH, start_heads, 0)

    lane = lax.broadcasted_iota(jnp.int32, (1, ROWS), 1)
    pos_q = jnp.where(
        lane < 64, ord_ref[0, 2 * ctx] * 64 + lane, ord_ref[0, 2 * ctx + 1] * 64 + lane - 64
    )
    start_q = jnp.zeros((1, ROWS), jnp.int32)
    end = jnp.int32(0)
    for j in range(8):
        end = end + doc_ref[0, j]
        start_q = jnp.where(pos_q >= end, end, start_q)
    for j in range(16):
        pos_n = ord_ref[0, j] * 64 + lax.broadcasted_iota(jnp.int32, (64, ROWS), 0)
        seen = (pos_n <= pos_q) & (pos_n >= start_q)
        cap[j * 64:(j + 1) * 64, :] = jnp.where(seen, BIG, -BIG)

    each(0, -K1, keys[1])
    each(0, -V0, values[0])
    load_hidden.wait()
    load_lse.wait()
    each(0, -K2, keys[2])
    each(0, -V1, values[1])
    each(0, -V2, values[2])

    def rows_of(g):
        wait(kvb.at[pl.ds(0, 3), 0], hsem.at[g])
        heads = lse[rng(g * GRP, GRP), :] * LOG2E
        for h in range(GRP):
            cols = slice(h * ROWS, (h + 1) * ROWS)
            prod = dob[g, :, cols].astype(F32) * ob[g, :, cols].astype(F32)
            deltar[g, :, cols] = jnp.sum(prod.T, axis=0, keepdims=True) * SCALE
            lser[g, :, cols] = heads[h:h + 1, :]

    def stack(ref, g):
        return jnp.concatenate([ref[g, :, h * HD:(h + 1) * HD] for h in range(GRP)], axis=0)

    def pass1(g):
        qq, dd = stack(qb, g), stack(dob, g)

        def block(nb, c):
            r = rng(nb * NB, NB)
            top = jnp.concatenate([cap[r, :]] * GRP, axis=1)
            st = dot(kvb[g, 0, r, :], qq, 1, 1)
            p = jnp.exp2(jnp.minimum(st * (SCALE * LOG2E) - lser[g], top)).astype(BF16)
            probs[g, r, :] = p
            pf[g, r, :] = dot(p, dd, 1, 0)
            return c

        lax.fori_loop(0, SEQ // NB, block, 0)

    def pass2(g):
        qq, dd = stack(qb, g), stack(dob, g)

        def block(nb):
            r = rng(nb * NB, NB)
            dp_ = dot(kvb[g, 1, r, :], dd, 1, 1)
            ds = (probs[g, r, :].astype(F32) * (dp_ * SCALE - deltar[g])).astype(BF16)
            pf[g, r, :] = dot(ds, qq, 1, 0)
            dqt[...] = (dqt[...] if nb else 0.0) + dot(kvb[g, 0, r, :].T, ds, 1, 0)

        for nb in range(SEQ // NB):
            block(nb)
        for h in range(GRP):
            cols = slice(h * ROWS, (h + 1) * ROWS)
            ob[g, :, cols] = dqt[:, cols].T.astype(BF16)
        dq_copy(g).start()

    def dq_copy(g):
        return pltpu.make_async_copy(ob.at[g], dq_ref.at[0, :, rng(g * GRP * HD, GRP * HD)], dqsem.at[0])

    def b1(w, g):
        j = w * 4 + g // 2
        s1[j, 0] = pf[g, half(yo, 0), :].astype(BF16)
        s1[j, 1] = pf[g, half(yo, 1), :].astype(BF16)
        go(w, g, B1P, B1M)

    def b2(w, g):
        j = w * 4 + g // 2
        s2[j, 0, ROWS:, :] = pf[g, half(yp, 1), :].astype(BF16)
        s2[j, 1, :ROWS, :] = pf[g, half(ym, 0), :].astype(BF16)
        take(w, g, B1P, 2 * ROWS)
        s2[j, 0, :ROWS, :] = (pf[g, half(yp, 0), :] + r1[j, 0].astype(F32)).astype(BF16)
        go(w, g, B2P)
        s2[j, 1, ROWS:, :] = (pf[g, half(ym, 1), :] + r1[j, 1].astype(F32)).astype(BF16)
        go(w, g, B2M)

    def b3(w, g):
        j = w * 4 + g // 2
        take(w, g, B2P, 4 * ROWS)

        def total(z):
            rows = rng(z * ROWS, ROWS)
            return pf[g, half(y, z), :] + r2[j, 0, rows, :].astype(F32) + r2[j, 1, rows, :].astype(F32)

        s3[j] = total(1 - zh).astype(BF16)
        go(w, g, B3)
        fin[j] = total(zh)

    def b4(w, g):
        j = w * 4 + g // 2
        take(w, g, B3, ROWS)
        result(w, g, fin[j] + r3[j].astype(F32))

    def w1(w, g):
        j = w * 4 + g // 2
        for s in range(4):
            w0s[j, s] = pf[g, half(s, 1 - zh), :].astype(BF16)
        go(w, g, W0)

    def w2(w, g):
        j = w * 4 + g // 2
        take(w, g, W0, 4 * ROWS)
        for s in range(4):
            pf[g, half(s, zh), :] += w0r[j, s].astype(F32)
        w1s[j, 0] = pf[g, quarter(yo, zh, 0), :].astype(BF16)
        w1s[j, 1] = pf[g, quarter(yo, zh, 1), :].astype(BF16)
        go(w, g, W1P, W1M)

    def w3(w, g):
        j = w * 4 + g // 2
        w2s[j, 0, 64:, :] = pf[g, quarter(yp, zh, 1), :].astype(BF16)
        w2s[j, 1, :64, :] = pf[g, quarter(ym, zh, 0), :].astype(BF16)
        take(w, g, W1P, ROWS)
        w2s[j, 0, :64, :] = (pf[g, quarter(yp, zh, 0), :] + w1r[j, 0].astype(F32)).astype(BF16)
        go(w, g, W2P)
        w2s[j, 1, 64:, :] = (pf[g, quarter(ym, zh, 1), :] + w1r[j, 1].astype(F32)).astype(BF16)
        go(w, g, W2M)

    def w4(w, g):
        j = w * 4 + g // 2
        take(w, g, W2P, 2 * ROWS)
        result(w, g, pf[g, own, :] + w2r[j, 0].astype(F32) + w2r[j, 1].astype(F32))

    def result(w, g, total):
        total = total.astype(BF16)
        if w:
            dk_ref[0, :, rng(g * HD, HD)] = total
        else:
            dv_ref[0, :, rng(g * HD, HD)] = total
            vgb[g // 2, rng(me * ROWS, ROWS), rng(lax.rem(g, 2) * HD, HD)] = total

    dv = [None] + [either(0, *two) for two in ((b1, w1), (b2, w2), (b3, w3), (b4, w4))]
    dk = [None] + [either(1, *two) for two in ((b1, w1), (b2, w2), (b3, w3), (b4, w4))]

    def send_h(k, z):
        xx, cc, to = near(k)
        return pltpu.make_async_remote_copy(
            src_ref=ht.at[rng(((xx * 2 + z) * 2 + cc) * 320, 320)],
            dst_ref=hg.at[z, :, rng(me * ROWS, ROWS)],
            send_sem=hs.at[0], recv_sem=hr.at[0], device_id=to, device_id_type=MESH,
        )

    def turn(i):
        dx, z = i // 2, lax.rem(i, 2)
        j = lax.rem(x + dx, 4) * 2 + z
        for n in range(5):
            at = j * 640 + n * 128
            ht[rng(at, 128), :] = hid[:, rng(at, 128)].T
        send_h(dx * 2 + 1, z).start()

        @pl.when(dx > 0)
        def _():
            send_h(dx * 2, z).start()

        @pl.when(dx == 0)
        def _():
            hg[z, :, rng(me * ROWS, ROWS)] = ht[rng((j * 2 + core) * 320, 320), :]

    def send_v(k, p):
        rows = rng(me * ROWS, ROWS)
        return pltpu.make_async_remote_copy(
            src_ref=vgb.at[p, rows], dst_ref=vgb.at[p, rows], send_sem=vs.at[0], recv_sem=vr.at[p],
            device_id=near(k)[2], device_id_type=MESH,
        )

    def send_w(k, p):
        yy, to = along_y(k)
        return pltpu.make_async_remote_copy(
            src_ref=dws.at[p, yy], dst_ref=dwr.at[p, k], send_sem=ws.at[0], recv_sem=wr.at[p],
            device_id=to, device_id_type=MESH,
        )

    def send_u(k, p):
        t, to = along_z(k)
        return pltpu.make_async_remote_copy(
            src_ref=dus.at[p, t], dst_ref=dur.at[p, k], send_sem=us.at[0], recv_sem=ur.at[p],
            device_id=to, device_id_type=MESH,
        )

    def weights1(p):
        each(1, 8, lambda k: send_v(k, p).start())

    def weights2(p):
        @pl.when(p == 0)
        def _():
            wait(hg.at[:, :, pl.ds(0, 7 * ROWS)], hr.at[0])

        wait(vgb.at[p, pl.ds(0, 7 * ROWS)], vr.at[p])
        res = dot(hg[...].reshape(640, SEQ), vgb[p], 1, 0).reshape(16, 40, 256)
        res = jnp.concatenate([res[:, :, :128], res[:, :, 128:]], axis=1).astype(BF16)
        for t in range(16):
            dws[p, (t // 2) % 4, t // 8 * 2 + t % 2] = res[t]
        each(1, 4, lambda k: send_w(k, p).start())

    def weights3(p):
        wait(dwr.at[p, pl.ds(0, 3)], wr.at[p])
        acc = dws[p, y].astype(F32)
        for k in range(1, 4):
            acc = acc + dwr[p, k].astype(F32)
        dus[p] = acc.astype(BF16)
        each(1, 4, lambda k: send_u(k, p).start())

    def weights4(p):
        wait(dur.at[p, pl.ds(0, 3)], ur.at[p])
        acc = dus[p, mine].astype(F32)
        for k in range(1, 4):
            acc = acc + dur[p, k].astype(F32)
        dw_ref[:, rng(p * 256, 128)] = acc[:40]
        dw_ref[:, rng(p * 256 + 128, 128)] = acc[40:]

    def at(i, lo, count, f):
        @pl.when((i >= lo) & (i < lo + count))
        def _():
            f(i - lo)

    def at_pair(i, lo, f):
        @pl.when((i >= lo) & (i < lo + 8) & (lax.rem(i - lo, 2) == 0))
        def _():
            f((i - lo) // 2)

    def step(i, c):
        at(i, K1, KVH, keys[1])
        at(i, K2, KVH, keys[2])
        at(i, V0, KVH, values[0])
        at(i, V1, KVH, values[1])
        at(i, V2, KVH, values[2])

        @pl.when(i < KVH)
        def _():
            rows_of(i)
            keys[3](i)
            pass1(i)
            dv[1](i)

        at(i, D2, KVH, dv[2])
        at(i, D3, KVH, dv[3])
        at(i, D4, KVH, dv[4])
        at_pair(i, G1, weights1)

        @pl.when(i < 4)
        def _():
            turn(2 * i)
            turn(2 * i + 1)

        @pl.when((i >= KVH) & (i < 2 * KVH))
        def _():
            g = i - KVH
            values[3](g)
            pass2(g)
            dk[1](g)

        at(i, E2, KVH, dk[2])
        at(i, E3, KVH, dk[3])
        at(i, E4, KVH, dk[4])
        at_pair(i, G2, weights2)
        at_pair(i, G3, weights3)
        at_pair(i, G4, weights4)
        return c

    lax.fori_loop(0, E4 + KVH, step, 0)

    every = kvb.at[:, 0, pl.ds(0, SENT)]
    for w in range(2):
        for n in range(2):
            wait(every, send.at[w, n])
    wait(ob, dqsem.at[0])
    wait(hg.at[:, :, pl.ds(0, 7 * ROWS)], hs.at[0])
    wait(vgb.at[:, pl.ds(0, 7 * ROWS)], vs.at[0])
    wait(dws.at[:, pl.ds(0, 3)], ws.at[0])
    wait(dus.at[:, pl.ds(0, 3)], us.at[0])


def copy_out(dq, dk, dv, dw, dq_out, dk_out, dv_out, dw_out, dq_v, dk_v, dv_v, dw_v, into, out):
    parts = [(dk, dk_v, dk_out), (dv, dv_v, dv_out), (dw, dw_v, dw_out)]
    for n in range(8):
        cols = pl.ds(n * 1024, 1024)
        parts.append((dq.at[:, :, cols], dq_v.at[n], dq_out.at[:, :, cols]))
    reads = [pltpu.make_async_copy(a, b, into.at[n]) for n, (a, b, _) in enumerate(parts)]
    writes = [pltpu.make_async_copy(b, c, out.at[n]) for n, (_, b, c) in enumerate(parts)]
    for copy in reads:
        copy.start()
    for read, write in zip(reads, writes):
        read.wait()
        write.start()
    for copy in writes:
        copy.wait()


def body(hidden, q, k, v, o, do, lse, docs, order):
    anyspace = pl.BlockSpec(memory_space=pl.ANY)
    vmem = pl.BlockSpec(memory_space=pltpu.VMEM)
    smem = pl.BlockSpec(memory_space=pltpu.SMEM)
    dma = pltpu.SemaphoreType.DMA
    shapes = (
        jax.ShapeDtypeStruct((1, ROWS, KVH * GRP * HD), BF16),
        jax.ShapeDtypeStruct((1, ROWS, KVH * HD), BF16),
        jax.ShapeDtypeStruct((1, ROWS, KVH * HD), BF16),
        jax.ShapeDtypeStruct((40, KVH * HD), F32),
    )
    results = pl.pallas_call(
        kernel,
        out_shape=shapes,
        in_specs=[smem, smem] + [anyspace] * 7,
        out_specs=(anyspace, vmem, vmem, vmem),
        scratch_shapes=[
            pltpu.VMEM((KVH, 2, SEQ, HD), BF16),
            pltpu.VMEM((KVH, ROWS, GRP * HD), BF16),
            pltpu.VMEM((KVH, ROWS, GRP * HD), BF16),
            pltpu.VMEM((KVH, ROWS, GRP * HD), BF16),
            pltpu.VMEM((SEQ, ROWS), F32),
            pltpu.VMEM((KVH, 1, GRP * ROWS), F32),
            pltpu.VMEM((KVH, 1, GRP * ROWS), F32),
            pltpu.VMEM((KVH, SEQ, HD), F32),
            pltpu.VMEM((HD, GRP * ROWS), F32),
            pltpu.VMEM((KVH, SEQ, GRP * ROWS), BF16),
            pltpu.VMEM((KVH * GRP, ROWS), F32),
            pltpu.VMEM((KVH, 2, ROWS, HD), BF16),
            pltpu.VMEM((KVH, 2, ROWS, HD), BF16),
            pltpu.VMEM((KVH, 2, 2 * ROWS, HD), BF16),
            pltpu.VMEM((KVH, 2, 2 * ROWS, HD), BF16),
            pltpu.VMEM((KVH, ROWS, HD), BF16),
            pltpu.VMEM((KVH, ROWS, HD), BF16),
            pltpu.VMEM((KVH, ROWS, HD), F32),
            pltpu.VMEM((KVH, 4, ROWS, HD), BF16),
            pltpu.VMEM((KVH, 4, ROWS, HD), BF16),
            pltpu.VMEM((KVH, 2, 64, HD), BF16),
            pltpu.VMEM((KVH, 2, 64, HD), BF16),
            pltpu.VMEM((KVH, 2, ROWS, HD), BF16),
            pltpu.VMEM((KVH, 2, ROWS, HD), BF16),
            pltpu.VMEM((ROWS, 5120), BF16),
            pltpu.VMEM((5120, ROWS), BF16),
            pltpu.VMEM((2, 320, SEQ), BF16),
            pltpu.VMEM((4, SEQ, 256), BF16),
            pltpu.VMEM((4, 4, 4, 80, 128), BF16),
            pltpu.VMEM((4, 4, 4, 80, 128), BF16),
            pltpu.VMEM((4, 4, 80, 128), BF16),
            pltpu.VMEM((4, 4, 80, 128), BF16),
            dma((2, 2)), dma((6, 2 * KVH)), dma((3,)), dma((KVH,)), dma((1,)),
            dma((1,)), dma((1,)), dma((1,)), dma((4,)), dma((1,)), dma((4,)), dma((1,)), dma((4,)),
        ],
        compiler_params=pltpu.CompilerParams(
            collective_id=0, has_side_effects=True, vmem_limit_bytes=62 * 2**20
        ),
        name="attention_and_weights",
    )(docs, order, q, k, v, o, do, lse, hidden)
    return pl.pallas_call(
        copy_out,
        out_shape=shapes,
        in_specs=[anyspace] * 4,
        out_specs=(anyspace,) * 4,
        scratch_shapes=[
            pltpu.VMEM((8, 1, ROWS, 1024), BF16),
            pltpu.VMEM((1, ROWS, KVH * HD), BF16),
            pltpu.VMEM((1, ROWS, KVH * HD), BF16),
            pltpu.VMEM((40, KVH * HD), F32),
            dma((11,)), dma((11,)),
        ],
        name="copy_out",
    )(*results)


def solution(mesh):
    placed = (P("dp", "ctx", None),) * 6 + (P("dp", None, "ctx"), P("dp", None), P("dp", None))
    return jax.shard_map(
        body,
        mesh=mesh,
        in_specs=placed,
        out_specs=(P("dp", "ctx", None),) * 3 + (P(("dp", "ctx"), None),),
        check_vma=False,
    )
```

```python
import math

import jax
import jax.numpy as jnp
from jax import lax
from jax.experimental import pallas as pl
from jax.experimental.pallas import tpu as pltpu
from jax.sharding import PartitionSpec as P

MESH = pl.DeviceIdType.MESH
F32 = jnp.float32
BF16 = jnp.bfloat16
KVH = 8
GRP = 8
HD = 128
ROWS = 128
SEQ = 1024
SCALE = HD ** (-0.5)
LOG2E = math.log2(math.e)
BIG = 3.0e38
NB = 1024
K1, K2, V0, V1, V2 = (-8, 1), (-4, 1), (0, 1), (3, 1), (6, 1)
P1, P2 = (0, 1), (8, 1)
D2, D3, D4 = (3, 1), (6, 1), (8, 1)
E2, E3, E4 = (11, 1), (14, 1), (17, 1)
G1, GB, G2, G3, G4 = (9, 2), (10, 2), (11, 2), (13, 2), (15, 2)
TICKS = 25

A0, A1P, A1M, A3P, A3M = range(5)
V1P, V1M, V2P, V2M, Z0, ZP, ZM, ZO = range(5, 13)
B1P, B1M, B2P, B2M, B3 = range(13, 18)
W0, W1P, W1M, W2P, W2M = range(18, 23)
SEM = (0, 1, 1, 2, 2) + (0, 0, 1, 1, 2, 2, 2, 2) + (3, 3, 4, 4, 5) + (3, 4, 4, 5, 5)
SENT = 896


def dot(a, b, ca, cb):
    return lax.dot_general(a, b, (((ca,), (cb,)), ((), ())), preferred_element_type=F32)


def rng(start, size):
    return pl.ds(pl.multiple_of(start, size), size)


def kernel(
    doc_ref, ord_ref, q_ref, k_ref, v_ref, o_ref, do_ref, lse_ref, h_ref,
    dq_ref, dk_ref, dv_ref, dw_ref,
    kvb, qb, dob, ob, cap, lser, deltar, pf, dqt, lse,
    s1, r1, s2, r2, s3, r3, fin, w0s, w0r, w1s, w1r, w2s, w2r,
    hid, ht, hg, vgb, dws, dwr, dus, dur,
    send, recv, lsem, hsem, dqsem, hs, hr, vs, vr, vc, ws, wr, us, ur,
):
    dp, ctx = lax.axis_index("dp"), lax.axis_index("ctx")
    x, zl, core = dp // 4, lax.rem(dp // 2, 2), lax.rem(dp, 2)
    y, zh = ctx // 2, lax.rem(ctx, 2)
    partner = y * 2 + 1 - zh
    yp, ym, yo = lax.rem(y + 1, 4), lax.rem(y + 3, 4), lax.rem(y + 2, 4)
    up, down = yp * 2 + zh, ym * 2 + zh
    me = x * 2 + core
    mine = zl * 2 + zh

    def near(k):
        xx, cc = lax.rem(x + k // 2, 4), lax.rem(core + lax.rem(k, 2), 2)
        return xx, cc, {"dp": (xx * 2 + zl) * 2 + cc}

    def along_y(k):
        yy = lax.rem(y + k, 4)
        return yy, {"ctx": yy * 2 + zh}

    def along_z(k):
        zz, hh = lax.rem(zl + k // 2, 2), lax.rem(zh + lax.rem(k, 2), 2)
        return zz * 2 + hh, {"dp": (x * 2 + zz) * 2 + core, "ctx": y * 2 + hh}

    barrier = pltpu.get_barrier_semaphore()
    for k in range(1, 8):
        pl.semaphore_signal(barrier, inc=1, device_id=near(k)[2], device_id_type=MESH)
    for k in range(1, 4):
        pl.semaphore_signal(barrier, inc=1, device_id=along_y(k)[1], device_id_type=MESH)
        pl.semaphore_signal(barrier, inc=1, device_id=along_z(k)[1], device_id_type=MESH)
    def load_kv(g, c):
        cols, rows = rng(g * HD, HD), rng(ctx * ROWS, ROWS)
        pltpu.make_async_copy(k_ref.at[0, :, cols], kvb.at[g, 0, rows], lsem.at[0]).start()
        pltpu.make_async_copy(v_ref.at[0, :, cols], kvb.at[g, 1, rows], lsem.at[0]).start()
        return c

    lax.fori_loop(0, KVH, load_kv, 0)

    own = rng(ctx * ROWS, ROWS)
    pltpu.make_async_copy(kvb.at[:, :, own], kvb.at[:, :, own], lsem.at[0]).wait()
    pl.semaphore_wait(barrier, 13)

    def slot(s):
        return rng(s * 2 * ROWS, 2 * ROWS)

    def half(s, z):
        return rng((s * 2 + z) * ROWS, ROWS)

    def quarter(s, z, n):
        return rng((s * 4 + z * 2 + n) * 64, 64)

    def msg(kind, w, g):
        same = {
            A0: (own, partner),
            A1P: (slot(y), up),
            A1M: (slot(y), down),
            A3P: (half(ym, 0), up),
            A3M: (half(yp, 1), down),
            V1P: (own, up),
            V1M: (own, down),
            V2P: (quarter(ym, zh, 0), up),
            V2M: (quarter(yp, zh, 1), down),
            Z0: (own, partner),
            ZP: (half(yp, zh), partner),
            ZM: (half(ym, zh), partner),
            ZO: (half(yo, zh), partner),
        }
        j = w * KVH + g
        other = {
            B1P: (s1.at[j, 0], r1.at[j, 0], up),
            B1M: (s1.at[j, 1], r1.at[j, 1], down),
            B2P: (s2.at[j, 0], r2.at[j, 0], up),
            B2M: (s2.at[j, 1], r2.at[j, 1], down),
            B3: (s3.at[j], r3.at[j], partner),
            W0: (w0s.at[j], w0r.at[j], partner),
            W1P: (w1s.at[j, 0], w1r.at[j, 0], up),
            W1M: (w1s.at[j, 1], w1r.at[j, 1], down),
            W2P: (w2s.at[j, 0], w2r.at[j, 0], up),
            W2M: (w2s.at[j, 1], w2r.at[j, 1], down),
        }
        if kind in same:
            rows, to = same[kind]
            src = dst = kvb.at[g, w, rows]
        else:
            src, dst, to = other[kind]
        return pltpu.make_async_remote_copy(
            src_ref=src, dst_ref=dst, send_sem=send.at[w, kind // 13], recv_sem=recv.at[SEM[kind], w * KVH + g],
            device_id={"ctx": to}, device_id_type=MESH,
        )

    def go(w, g, *kinds):
        for kind in kinds:
            msg(kind, w, g).start()

    def take(w, g, kind, rows):
        whole = kvb.at[g, w, pl.ds(0, rows)]
        pltpu.make_async_copy(whole, whole, recv.at[SEM[kind], w * KVH + g]).wait()

    def wait(ref, sem):
        pltpu.make_async_copy(ref, ref, sem).wait()

    def each(lo, hi, f):
        def one(k, c):
            f(k)
            return c

        lax.fori_loop(lo, hi, one, 0)

    def either(w, first, second):
        def run(g):
            most = lax.rem(g * 5 + w * 4, 8) < 5

            @pl.when(most)
            def _():
                first(w, g)

            @pl.when(jnp.logical_not(most))
            def _():
                second(w, g)

        return run

    def zy0(w, g):
        go(w, g, A0)

    def zy1(w, g):
        take(w, g, A0, ROWS)
        go(w, g, A1P, A1M)

    def zy2(w, g):
        take(w, g, A1P, 4 * ROWS)
        go(w, g, A3P, A3M)

    def zy3(w, g):
        take(w, g, A3P, 2 * ROWS)

    def yz0(w, g):
        go(w, g, V1P, V1M, Z0)

    def yz1(w, g):
        take(w, g, V1P, 2 * ROWS)
        go(w, g, V2P, V2M, ZM, ZP)

    def yz2(w, g):
        take(w, g, V2P, ROWS)
        go(w, g, ZO)

    def yz3(w, g):
        take(w, g, Z0, 4 * ROWS)

    keys = [either(0, *two) for two in ((zy0, yz0), (zy1, yz1), (zy2, yz2), (zy3, yz3))]
    values = [either(1, *two) for two in ((zy0, yz0), (zy1, yz1), (zy2, yz2), (zy3, yz3))]

    each(0, KVH, keys[0])

    load_lse = pltpu.make_async_copy(lse_ref.at[0], lse, lsem.at[2])
    load_lse.start()
    load_hidden = pltpu.make_async_copy(h_ref.at[0], hid, lsem.at[1])
    load_hidden.start()

    def load_heads(g):
        cols = rng(g * GRP * HD, GRP * HD)
        return [
            pltpu.make_async_copy(ref.at[0, :, cols], buf.at[g], hsem.at[g])
            for ref, buf in ((do_ref, dob), (o_ref, ob), (q_ref, qb))
        ]

    def start_heads(g, c):
        for copy in load_heads(g):
            copy.start()
        return c

    lax.fori_loop(0, KVH, start_heads, 0)

    lane = lax.broadcasted_iota(jnp.int32, (1, ROWS), 1)
    pos_q = jnp.where(
        lane < 64, ord_ref[0, 2 * ctx] * 64 + lane, ord_ref[0, 2 * ctx + 1] * 64 + lane - 64
    )
    start_q = jnp.zeros((1, ROWS), jnp.int32)
    end = jnp.int32(0)
    for j in range(8):
        end = end + doc_ref[0, j]
        start_q = jnp.where(pos_q >= end, end, start_q)
    for j in range(16):
        pos_n = ord_ref[0, j] * 64 + lax.broadcasted_iota(jnp.int32, (64, ROWS), 0)
        seen = (pos_n <= pos_q) & (pos_n >= start_q)
        cap[j * 64:(j + 1) * 64, :] = jnp.where(seen, BIG, -BIG)

    each(0, -K1[0], keys[1])
    each(0, -min(V0[0], 0), values[0])
    load_hidden.wait()
    load_lse.wait()
    each(0, -K2[0], keys[2])

    def rows_of(g):
        wait(kvb.at[pl.ds(0, 3), 0], hsem.at[g])
        heads = lse[rng(g * GRP, GRP), :] * LOG2E
        for h in range(GRP):
            cols = slice(h * ROWS, (h + 1) * ROWS)
            prod = dob[g, :, cols].astype(F32) * ob[g, :, cols].astype(F32)
            deltar[g, :, cols] = jnp.sum(prod.T, axis=0, keepdims=True) * SCALE
            lser[g, :, cols] = heads[h:h + 1, :]

    def stack(ref, g):
        return jnp.concatenate([ref[g, :, h * HD:(h + 1) * HD] for h in range(GRP)], axis=0)

    def probs(g, r, qq):
        top = jnp.concatenate([cap[r, :]] * GRP, axis=1)
        st = dot(kvb[g, 0, r, :], qq, 1, 1)
        return jnp.exp2(jnp.minimum(st * (SCALE * LOG2E) - lser[g], top))

    def pass1(g):
        qq, dd = stack(qb, g), stack(dob, g)

        def block(nb, c):
            r = rng(nb * NB, NB)
            p = probs(g, r, qq).astype(BF16)
            pf[0, g, r, :] = dot(p, dd, 1, 0)
            return c

        lax.fori_loop(0, SEQ // NB, block, 0)

    def pass2(g):
        qq, dd = stack(qb, g), stack(dob, g)

        def block(nb):
            r = rng(nb * NB, NB)
            p = probs(g, r, qq)
            dp_ = dot(kvb[g, 1, r, :], dd, 1, 1)
            ds = (p * (dp_ * SCALE - deltar[g])).astype(BF16)
            pf[1, g, r, :] = dot(ds, qq, 1, 0)
            dqt[...] = (dqt[...] if nb else 0.0) + dot(kvb[g, 0, r, :].T, ds, 1, 0)

        for nb in range(SEQ // NB):
            block(nb)
        for h in range(GRP):
            cols = slice(h * ROWS, (h + 1) * ROWS)
            ob[g, :, cols] = dqt[:, cols].T.astype(BF16)
        dq_copy(g).start()

    def dq_copy(g):
        return pltpu.make_async_copy(ob.at[g], dq_ref.at[0, :, rng(g * GRP * HD, GRP * HD)], dqsem.at[0])

    def b1(w, g):
        j = w * KVH + g
        s1[j, 0] = pf[w, g, half(yo, 0), :].astype(BF16)
        s1[j, 1] = pf[w, g, half(yo, 1), :].astype(BF16)
        go(w, g, B1P, B1M)

    def b2(w, g):
        j = w * KVH + g
        s2[j, 0, ROWS:, :] = pf[w, g, half(yp, 1), :].astype(BF16)
        s2[j, 1, :ROWS, :] = pf[w, g, half(ym, 0), :].astype(BF16)
        take(w, g, B1P, 2 * ROWS)
        s2[j, 0, :ROWS, :] = (pf[w, g, half(yp, 0), :] + r1[j, 0].astype(F32)).astype(BF16)
        go(w, g, B2P)
        s2[j, 1, ROWS:, :] = (pf[w, g, half(ym, 1), :] + r1[j, 1].astype(F32)).astype(BF16)
        go(w, g, B2M)

    def b3(w, g):
        j = w * KVH + g
        take(w, g, B2P, 4 * ROWS)

        def total(z):
            rows = rng(z * ROWS, ROWS)
            return pf[w, g, half(y, z), :] + r2[j, 0, rows, :].astype(F32) + r2[j, 1, rows, :].astype(F32)

        s3[j] = total(1 - zh).astype(BF16)
        go(w, g, B3)
        fin[j] = total(zh)

    def b4(w, g):
        j = w * KVH + g
        take(w, g, B3, ROWS)
        result(w, g, fin[j] + r3[j].astype(F32))

    def w1(w, g):
        j = w * KVH + g
        for s in range(4):
            w0s[j, s] = pf[w, g, half(s, 1 - zh), :].astype(BF16)
        go(w, g, W0)

    def w2(w, g):
        j = w * KVH + g
        take(w, g, W0, 4 * ROWS)
        for s in range(4):
            pf[w, g, half(s, zh), :] += w0r[j, s].astype(F32)
        w1s[j, 0] = pf[w, g, quarter(yo, zh, 0), :].astype(BF16)
        w1s[j, 1] = pf[w, g, quarter(yo, zh, 1), :].astype(BF16)
        go(w, g, W1P, W1M)

    def w3(w, g):
        j = w * KVH + g
        w2s[j, 0, 64:, :] = pf[w, g, quarter(yp, zh, 1), :].astype(BF16)
        w2s[j, 1, :64, :] = pf[w, g, quarter(ym, zh, 0), :].astype(BF16)
        take(w, g, W1P, ROWS)
        w2s[j, 0, :64, :] = (pf[w, g, quarter(yp, zh, 0), :] + w1r[j, 0].astype(F32)).astype(BF16)
        go(w, g, W2P)
        w2s[j, 1, 64:, :] = (pf[w, g, quarter(ym, zh, 1), :] + w1r[j, 1].astype(F32)).astype(BF16)
        go(w, g, W2M)

    def w4(w, g):
        j = w * KVH + g
        take(w, g, W2P, 2 * ROWS)
        result(w, g, pf[w, g, own, :] + w2r[j, 0].astype(F32) + w2r[j, 1].astype(F32))

    def result(w, g, total):
        total = total.astype(BF16)
        if w:
            dk_ref[0, :, rng(g * HD, HD)] = total
        else:
            dv_ref[0, :, rng(g * HD, HD)] = total
            vgb[g // 2, rng(me * ROWS, ROWS), rng(lax.rem(g, 2) * HD, HD)] = total

    dv = [None] + [either(0, *two) for two in ((b1, w1), (b2, w2), (b3, w3), (b4, w4))]
    dk = [None] + [either(1, *two) for two in ((b1, w1), (b2, w2), (b3, w3), (b4, w4))]

    def send_h(k, z):
        xx, cc, to = near(k)
        return pltpu.make_async_remote_copy(
            src_ref=ht.at[rng(((xx * 2 + z) * 2 + cc) * 320, 320)],
            dst_ref=hg.at[z, :, rng(me * ROWS, ROWS)],
            send_sem=hs.at[0], recv_sem=hr.at[0], device_id=to, device_id_type=MESH,
        )

    def turn(i):
        dx, z = i // 2, lax.rem(i, 2)
        j = lax.rem(x + dx, 4) * 2 + z
        for n in range(5):
            at = j * 640 + n * 128
            ht[rng(at, 128), :] = hid[:, rng(at, 128)].T
        send_h(dx * 2 + 1, z).start()

        @pl.when(dx > 0)
        def _():
            send_h(dx * 2, z).start()

        @pl.when(dx == 0)
        def _():
            hg[z, :, rng(me * ROWS, ROWS)] = ht[rng((j * 2 + core) * 320, 320), :]

    def send_v(k, p, n, sem):
        rows = rng((lax.rem(x + n, 4) * 2 + core) * ROWS, ROWS)
        return pltpu.make_async_remote_copy(
            src_ref=vgb.at[p, rows], dst_ref=vgb.at[p, rows], send_sem=vs.at[0], recv_sem=sem.at[p],
            device_id=near(k)[2], device_id_type=MESH,
        )

    def send_w(k, p):
        t, to = along_z(k)
        return pltpu.make_async_remote_copy(
            src_ref=dws.at[p, t], dst_ref=dwr.at[p, k], send_sem=ws.at[0], recv_sem=wr.at[p],
            device_id=to, device_id_type=MESH,
        )

    def send_u(k, p):
        yy, to = along_y(k)
        return pltpu.make_async_remote_copy(
            src_ref=dus.at[p, yy], dst_ref=dur.at[p, k], send_sem=us.at[0], recv_sem=ur.at[p],
            device_id=to, device_id_type=MESH,
        )

    def weights1(p):
        each(1, 4, lambda n: send_v(2 * n, p, 0, vr).start())
        send_v(1, p, 0, vc).start()

    def weights1b(p):
        wait(vgb.at[p, pl.ds(0, 3 * ROWS)], vr.at[p])
        each(1, 4, lambda n: send_v(1, p, n, vc).start())

    def weights2(p):
        @pl.when(p == 0)
        def _():
            wait(hg.at[:, :, pl.ds(0, 7 * ROWS)], hr.at[0])

        wait(vgb.at[p, pl.ds(0, 4 * ROWS)], vc.at[p])
        res = dot(hg[...].reshape(640, SEQ), vgb[p], 1, 0).reshape(16, 40, 256)
        res = jnp.concatenate([res[:, :, :128], res[:, :, 128:]], axis=1).astype(BF16)
        for t in range(16):
            dws[p, t // 8 * 2 + t % 2, (t // 2) % 4] = res[t]
        each(1, 4, lambda k: send_w(k, p).start())

    def weights3(p):
        wait(dwr.at[p, pl.ds(0, 3)], wr.at[p])
        acc = dws[p, mine].astype(F32)
        for k in range(1, 4):
            acc = acc + dwr[p, k].astype(F32)
        dus[p] = acc.astype(BF16)
        each(1, 4, lambda k: send_u(k, p).start())

    def weights4(p):
        wait(dur.at[p, pl.ds(0, 3)], ur.at[p])
        acc = dus[p, y].astype(F32)
        for k in range(1, 4):
            acc = acc + dur[p, k].astype(F32)
        dw_ref[:, rng(p * 256, 128)] = acc[:40]
        dw_ref[:, rng(p * 256 + 128, 128)] = acc[40:]

    def at(i, when, count, f):
        lo, stride = when
        n = i - lo

        @pl.when((n >= 0) & (n < count * stride) & (lax.rem(n, stride) == 0))
        def _():
            f(n // stride)

    def first(g):
        rows_of(g)
        keys[3](g)
        pass1(g)
        dv[1](g)

    def second(g):
        values[3](g)
        pass2(g)
        dk[1](g)

    def step(i, c):
        at(i, E4, KVH, dk[4])
        at(i, E3, KVH, dk[3])
        at(i, E2, KVH, dk[2])
        at(i, D4, KVH, dv[4])
        at(i, G1, 4, weights1)
        at(i, GB, 4, weights1b)
        at(i, G2, 4, weights2)
        at(i, G3, 4, weights3)
        at(i, G4, 4, weights4)
        at(i, D3, KVH, dv[3])
        at(i, D2, KVH, dv[2])
        at(i, K1, KVH, keys[1])
        at(i, K2, KVH, keys[2])
        at(i, V0, KVH, values[0])
        at(i, V1, KVH, values[1])
        at(i, V2, KVH, values[2])
        at(i, (0, 1), KVH, turn)
        at(i, P1, KVH, first)
        at(i, P2, KVH, second)
        return c

    lax.fori_loop(0, TICKS, step, 0)

    every = kvb.at[:, 0, pl.ds(0, SENT)]
    for w in range(2):
        for n in range(2):
            wait(every, send.at[w, n])
    wait(ob, dqsem.at[0])
    wait(hg.at[:, :, pl.ds(0, 7 * ROWS)], hs.at[0])
    wait(vgb.at[:, pl.ds(0, 7 * ROWS)], vs.at[0])
    wait(dws.at[:, pl.ds(0, 3)], ws.at[0])
    wait(dus.at[:, pl.ds(0, 3)], us.at[0])


def copy_out(dq, dk, dv, dw, dq_out, dk_out, dv_out, dw_out, dq_v, dk_v, dv_v, dw_v, into, out):
    parts = [(dk, dk_v, dk_out), (dv, dv_v, dv_out), (dw, dw_v, dw_out)]
    for n in range(8):
        cols = pl.ds(n * 1024, 1024)
        parts.append((dq.at[:, :, cols], dq_v.at[n], dq_out.at[:, :, cols]))
    reads = [pltpu.make_async_copy(a, b, into.at[n]) for n, (a, b, _) in enumerate(parts)]
    writes = [pltpu.make_async_copy(b, c, out.at[n]) for n, (_, b, c) in enumerate(parts)]
    for copy in reads:
        copy.start()
    for read, write in zip(reads, writes):
        read.wait()
        write.start()
    for copy in writes:
        copy.wait()


def body(hidden, q, k, v, o, do, lse, docs, order):
    anyspace = pl.BlockSpec(memory_space=pl.ANY)
    vmem = pl.BlockSpec(memory_space=pltpu.VMEM)
    smem = pl.BlockSpec(memory_space=pltpu.SMEM)
    dma = pltpu.SemaphoreType.DMA
    shapes = (
        jax.ShapeDtypeStruct((1, ROWS, KVH * GRP * HD), BF16),
        jax.ShapeDtypeStruct((1, ROWS, KVH * HD), BF16),
        jax.ShapeDtypeStruct((1, ROWS, KVH * HD), BF16),
        jax.ShapeDtypeStruct((40, KVH * HD), F32),
    )
    results = pl.pallas_call(
        kernel,
        out_shape=shapes,
        in_specs=[smem, smem] + [anyspace] * 7,
        out_specs=(anyspace, vmem, vmem, vmem),
        scratch_shapes=[
            pltpu.VMEM((KVH, 2, SEQ, HD), BF16),
            pltpu.VMEM((KVH, ROWS, GRP * HD), BF16),
            pltpu.VMEM((KVH, ROWS, GRP * HD), BF16),
            pltpu.VMEM((KVH, ROWS, GRP * HD), BF16),
            pltpu.VMEM((SEQ, ROWS), F32),
            pltpu.VMEM((KVH, 1, GRP * ROWS), F32),
            pltpu.VMEM((KVH, 1, GRP * ROWS), F32),
            pltpu.VMEM((2, KVH, SEQ, HD), F32),
            pltpu.VMEM((HD, GRP * ROWS), F32),
            pltpu.VMEM((KVH * GRP, ROWS), F32),
            pltpu.VMEM((2 * KVH, 2, ROWS, HD), BF16),
            pltpu.VMEM((2 * KVH, 2, ROWS, HD), BF16),
            pltpu.VMEM((2 * KVH, 2, 2 * ROWS, HD), BF16),
            pltpu.VMEM((2 * KVH, 2, 2 * ROWS, HD), BF16),
            pltpu.VMEM((2 * KVH, ROWS, HD), BF16),
            pltpu.VMEM((2 * KVH, ROWS, HD), BF16),
            pltpu.VMEM((2 * KVH, ROWS, HD), F32),
            pltpu.VMEM((2 * KVH, 4, ROWS, HD), BF16),
            pltpu.VMEM((2 * KVH, 4, ROWS, HD), BF16),
            pltpu.VMEM((2 * KVH, 2, 64, HD), BF16),
            pltpu.VMEM((2 * KVH, 2, 64, HD), BF16),
            pltpu.VMEM((2 * KVH, 2, ROWS, HD), BF16),
            pltpu.VMEM((2 * KVH, 2, ROWS, HD), BF16),
            pltpu.VMEM((ROWS, 5120), BF16),
            pltpu.VMEM((5120, ROWS), BF16),
            pltpu.VMEM((2, 320, SEQ), BF16),
            pltpu.VMEM((4, SEQ, 256), BF16),
            pltpu.VMEM((4, 4, 4, 80, 128), BF16),
            pltpu.VMEM((4, 4, 4, 80, 128), BF16),
            pltpu.VMEM((4, 4, 80, 128), BF16),
            pltpu.VMEM((4, 4, 80, 128), BF16),
            dma((2, 2)), dma((6, 2 * KVH)), dma((3,)), dma((KVH,)), dma((1,)),
            dma((1,)), dma((1,)), dma((1,)), dma((4,)), dma((4,)), dma((1,)), dma((4,)), dma((1,)), dma((4,)),
        ],
        compiler_params=pltpu.CompilerParams(
            collective_id=0, has_side_effects=True, vmem_limit_bytes=62 * 2**20
        ),
        name="attention_and_weights",
    )(docs, order, q, k, v, o, do, lse, hidden)
    return pl.pallas_call(
        copy_out,
        out_shape=shapes,
        in_specs=[anyspace] * 4,
        out_specs=(anyspace,) * 4,
        scratch_shapes=[
            pltpu.VMEM((8, 1, ROWS, 1024), BF16),
            pltpu.VMEM((1, ROWS, KVH * HD), BF16),
            pltpu.VMEM((1, ROWS, KVH * HD), BF16),
            pltpu.VMEM((40, KVH * HD), F32),
            dma((11,)), dma((11,)),
        ],
        name="copy_out",
    )(*results)


def solution(mesh):
    placed = (P("dp", "ctx", None),) * 6 + (P("dp", None, "ctx"), P("dp", None), P("dp", None))
    return jax.shard_map(
        body,
        mesh=mesh,
        in_specs=placed,
        out_specs=(P("dp", "ctx", None),) * 3 + (P(("dp", "ctx"), None),),
        check_vma=False,
    )
```

```python
import math

import jax
import jax.numpy as jnp
from jax import lax
from jax.experimental import pallas as pl
from jax.experimental.pallas import tpu as pltpu
from jax.sharding import PartitionSpec as P

MESH = pl.DeviceIdType.MESH
F32 = jnp.float32
BF16 = jnp.bfloat16
KVH = 8
GRP = 8
HD = 128
ROWS = 128
SEQ = 1024
SCALE = HD ** (-0.5)
LOG2E = math.log2(math.e)
BIG = 3.0e38
NB = 1024
K1, K2, V0, V1, V2 = (-8, 1), (-4, 1), (0, 1), (3, 1), (6, 1)
P1, P2 = (0, 1), (8, 1)
D2, D3, D4 = (3, 1), (6, 1), (8, 1)
E2, E3, E4 = (11, 1), (14, 1), (17, 1)
G1, GB, G2, G3, G4 = (9, 2), (10, 2), (11, 2), (13, 2), (15, 2)
TICKS = 25

A0, A1P, A1M, A3P, A3M = range(5)
V1P, V1M, V2P, V2M, Z0, ZP, ZM, ZO = range(5, 13)
B1P, B1M, B2P, B2M, B3 = range(13, 18)
W0, W1P, W1M, W2P, W2M = range(18, 23)
SEM = (0, 1, 1, 2, 2) + (0, 0, 1, 1, 2, 2, 2, 2) + (3, 3, 4, 4, 5) + (3, 4, 4, 5, 5)
SENT = 896


def dot(a, b, ca, cb):
    return lax.dot_general(a, b, (((ca,), (cb,)), ((), ())), preferred_element_type=F32)


def rng(start, size):
    return pl.ds(pl.multiple_of(start, size), size)


def kernel(
    doc_ref, ord_ref, q_ref, k_ref, v_ref, o_ref, do_ref, lse_ref, h_ref,
    dq_ref, dk_ref, dv_ref, dw_ref,
    kvb, qb, dob, ob, cap, lser, deltar, pf, dqt, lse,
    s1, r1, s2, r2, s3, r3, fin, w0s, w0r, w1s, w1r, w2s, w2r,
    hid, ht, hg, vgb, dws, dwr, dus, dur,
    send, recv, lsem, hsem, dqsem, hs, hr, vs, vr, vc, ws, wr, us, ur,
):
    dp, ctx = lax.axis_index("dp"), lax.axis_index("ctx")
    x, zl, core = dp // 4, lax.rem(dp // 2, 2), lax.rem(dp, 2)
    y, zh = ctx // 2, lax.rem(ctx, 2)
    partner = y * 2 + 1 - zh
    yp, ym, yo = lax.rem(y + 1, 4), lax.rem(y + 3, 4), lax.rem(y + 2, 4)
    up, down = yp * 2 + zh, ym * 2 + zh
    me = x * 2 + core
    mine = zl * 2 + zh

    def near(k):
        xx, cc = lax.rem(x + k // 2, 4), lax.rem(core + lax.rem(k, 2), 2)
        return xx, cc, {"dp": (xx * 2 + zl) * 2 + cc}

    def along_y(k):
        yy = lax.rem(y + k, 4)
        return yy, {"ctx": yy * 2 + zh}

    def along_z(k):
        zz, hh = lax.rem(zl + k // 2, 2), lax.rem(zh + lax.rem(k, 2), 2)
        return zz * 2 + hh, {"dp": (x * 2 + zz) * 2 + core, "ctx": y * 2 + hh}

    barrier = pltpu.get_barrier_semaphore()
    for k in range(1, 8):
        pl.semaphore_signal(barrier, inc=1, device_id=near(k)[2], device_id_type=MESH)
    for k in range(1, 4):
        pl.semaphore_signal(barrier, inc=1, device_id=along_y(k)[1], device_id_type=MESH)
        pl.semaphore_signal(barrier, inc=1, device_id=along_z(k)[1], device_id_type=MESH)
    def load_kv(g, c):
        cols, rows = rng(g * HD, HD), rng(ctx * ROWS, ROWS)
        pltpu.make_async_copy(k_ref.at[0, :, cols], kvb.at[g, 0, rows], lsem.at[0]).start()
        pltpu.make_async_copy(v_ref.at[0, :, cols], kvb.at[g, 1, rows], lsem.at[0]).start()
        return c

    lax.fori_loop(0, KVH, load_kv, 0)

    own = rng(ctx * ROWS, ROWS)
    pltpu.make_async_copy(kvb.at[:, :, own], kvb.at[:, :, own], lsem.at[0]).wait()
    pl.semaphore_wait(barrier, 13)

    def slot(s):
        return rng(s * 2 * ROWS, 2 * ROWS)

    def half(s, z):
        return rng((s * 2 + z) * ROWS, ROWS)

    def quarter(s, z, n):
        return rng((s * 4 + z * 2 + n) * 64, 64)

    def msg(kind, w, g):
        same = {
            A0: (own, partner),
            A1P: (slot(y), up),
            A1M: (slot(y), down),
            A3P: (half(ym, 0), up),
            A3M: (half(yp, 1), down),
            V1P: (own, up),
            V1M: (own, down),
            V2P: (quarter(ym, zh, 0), up),
            V2M: (quarter(yp, zh, 1), down),
            Z0: (own, partner),
            ZP: (half(yp, zh), partner),
            ZM: (half(ym, zh), partner),
            ZO: (half(yo, zh), partner),
        }
        j = w * KVH + g
        other = {
            B1P: (s1.at[j, 0], r1.at[j, 0], up),
            B1M: (s1.at[j, 1], r1.at[j, 1], down),
            B2P: (s2.at[j, 0], r2.at[j, 0], up),
            B2M: (s2.at[j, 1], r2.at[j, 1], down),
            B3: (s3.at[j], r3.at[j], partner),
            W0: (w0s.at[j], w0r.at[j], partner),
            W1P: (w1s.at[j, 0], w1r.at[j, 0], up),
            W1M: (w1s.at[j, 1], w1r.at[j, 1], down),
            W2P: (w2s.at[j, 0], w2r.at[j, 0], up),
            W2M: (w2s.at[j, 1], w2r.at[j, 1], down),
        }
        if kind in same:
            rows, to = same[kind]
            src = dst = kvb.at[g, w, rows]
        else:
            src, dst, to = other[kind]
        return pltpu.make_async_remote_copy(
            src_ref=src, dst_ref=dst, send_sem=send.at[w, kind // 13], recv_sem=recv.at[SEM[kind], w * KVH + g],
            device_id={"ctx": to}, device_id_type=MESH,
        )

    def go(w, g, *kinds):
        for kind in kinds:
            msg(kind, w, g).start()

    def take(w, g, kind, rows):
        whole = kvb.at[g, w, pl.ds(0, rows)]
        pltpu.make_async_copy(whole, whole, recv.at[SEM[kind], w * KVH + g]).wait()

    def wait(ref, sem):
        pltpu.make_async_copy(ref, ref, sem).wait()

    def each(lo, hi, f):
        def one(k, c):
            f(k)
            return c

        lax.fori_loop(lo, hi, one, 0)

    def either(w, first, second):
        def run(g):
            most = lax.rem(g * 5 + w * 4, 8) < 5

            @pl.when(most)
            def _():
                first(w, g)

            @pl.when(jnp.logical_not(most))
            def _():
                second(w, g)

        return run

    def zy0(w, g):
        go(w, g, A0)

    def zy1(w, g):
        take(w, g, A0, ROWS)
        go(w, g, A1P, A1M)

    def zy2(w, g):
        take(w, g, A1P, 4 * ROWS)
        go(w, g, A3P, A3M)

    def zy3(w, g):
        take(w, g, A3P, 2 * ROWS)

    def yz0(w, g):
        go(w, g, V1P, V1M, Z0)

    def yz1(w, g):
        take(w, g, V1P, 2 * ROWS)
        go(w, g, V2P, V2M, ZM, ZP)

    def yz2(w, g):
        take(w, g, V2P, ROWS)
        go(w, g, ZO)

    def yz3(w, g):
        take(w, g, Z0, 4 * ROWS)

    keys = [either(0, *two) for two in ((zy0, yz0), (zy1, yz1), (zy2, yz2), (zy3, yz3))]
    values = [either(1, *two) for two in ((zy0, yz0), (zy1, yz1), (zy2, yz2), (zy3, yz3))]

    each(0, KVH, keys[0])

    load_lse = pltpu.make_async_copy(lse_ref.at[0], lse, lsem.at[2])
    load_lse.start()
    load_hidden = pltpu.make_async_copy(h_ref.at[0], hid, lsem.at[1])
    load_hidden.start()

    def load_heads(g):
        cols = rng(g * GRP * HD, GRP * HD)
        return [
            pltpu.make_async_copy(ref.at[0, :, cols], buf.at[g], hsem.at[g])
            for ref, buf in ((do_ref, dob), (o_ref, ob), (q_ref, qb))
        ]

    def start_heads(g, c):
        for copy in load_heads(g):
            copy.start()
        return c

    lax.fori_loop(0, KVH, start_heads, 0)

    lane = lax.broadcasted_iota(jnp.int32, (1, ROWS), 1)
    pos_q = jnp.where(
        lane < 64, ord_ref[0, 2 * ctx] * 64 + lane, ord_ref[0, 2 * ctx + 1] * 64 + lane - 64
    )
    start_q = jnp.zeros((1, ROWS), jnp.int32)
    end = jnp.int32(0)
    for j in range(8):
        end = end + doc_ref[0, j]
        start_q = jnp.where(pos_q >= end, end, start_q)
    for j in range(16):
        pos_n = ord_ref[0, j] * 64 + lax.broadcasted_iota(jnp.int32, (64, ROWS), 0)
        seen = (pos_n <= pos_q) & (pos_n >= start_q)
        cap[j * 64:(j + 1) * 64, :] = jnp.where(seen, BIG, -BIG)

    each(0, -K1[0], keys[1])
    each(0, -min(V0[0], 0), values[0])
    load_hidden.wait()
    load_lse.wait()
    each(0, -K2[0], keys[2])

    def rows_of(g):
        wait(kvb.at[pl.ds(0, 3), 0], hsem.at[g])
        heads = lse[rng(g * GRP, GRP), :] * LOG2E
        for h in range(GRP):
            cols = slice(h * ROWS, (h + 1) * ROWS)
            prod = dob[g, :, cols].astype(F32) * ob[g, :, cols].astype(F32)
            deltar[g, :, cols] = jnp.sum(prod.T, axis=0, keepdims=True) * SCALE
            lser[g, :, cols] = heads[h:h + 1, :]

    def stack(ref, g):
        return jnp.concatenate([ref[g, :, h * HD:(h + 1) * HD] for h in range(GRP)], axis=0)

    def probs(g, r, qq):
        top = jnp.concatenate([cap[r, :]] * GRP, axis=1)
        st = dot(kvb[g, 0, r, :], qq, 1, 1)
        return jnp.exp2(jnp.minimum(st * (SCALE * LOG2E) - lser[g], top))

    def pass1(g):
        qq, dd = stack(qb, g), stack(dob, g)

        def block(nb, c):
            r = rng(nb * NB, NB)
            p = probs(g, r, qq).astype(BF16)
            pf[0, g, r, :] = dot(p, dd, 1, 0)
            return c

        lax.fori_loop(0, SEQ // NB, block, 0)

    def pass2(g):
        qq, dd = stack(qb, g), stack(dob, g)

        def block(nb):
            r = rng(nb * NB, NB)
            p = probs(g, r, qq)
            dp_ = dot(kvb[g, 1, r, :], dd, 1, 1)
            ds = (p * (dp_ * SCALE - deltar[g])).astype(BF16)
            pf[1, g, r, :] = dot(ds, qq, 1, 0)
            if nb == SEQ // NB - 1:
                dk[1](g)
            dqt[...] = (dqt[...] if nb else 0.0) + dot(kvb[g, 0, r, :].T, ds, 1, 0)

        for nb in range(SEQ // NB):
            block(nb)
        for h in range(GRP):
            cols = slice(h * ROWS, (h + 1) * ROWS)
            ob[g, :, cols] = dqt[:, cols].T.astype(BF16)
        dq_copy(g).start()

    def dq_copy(g):
        return pltpu.make_async_copy(ob.at[g], dq_ref.at[0, :, rng(g * GRP * HD, GRP * HD)], dqsem.at[0])

    def b1(w, g):
        j = w * KVH + g
        s1[j, 0] = pf[w, g, half(yo, 0), :].astype(BF16)
        s1[j, 1] = pf[w, g, half(yo, 1), :].astype(BF16)
        go(w, g, B1P, B1M)

    def b2(w, g):
        j = w * KVH + g
        s2[j, 0, ROWS:, :] = pf[w, g, half(yp, 1), :].astype(BF16)
        s2[j, 1, :ROWS, :] = pf[w, g, half(ym, 0), :].astype(BF16)
        take(w, g, B1P, 2 * ROWS)
        s2[j, 0, :ROWS, :] = (pf[w, g, half(yp, 0), :] + r1[j, 0].astype(F32)).astype(BF16)
        go(w, g, B2P)
        s2[j, 1, ROWS:, :] = (pf[w, g, half(ym, 1), :] + r1[j, 1].astype(F32)).astype(BF16)
        go(w, g, B2M)

    def b3(w, g):
        j = w * KVH + g
        take(w, g, B2P, 4 * ROWS)

        def total(z):
            rows = rng(z * ROWS, ROWS)
            return pf[w, g, half(y, z), :] + r2[j, 0, rows, :].astype(F32) + r2[j, 1, rows, :].astype(F32)

        s3[j] = total(1 - zh).astype(BF16)
        go(w, g, B3)
        fin[j] = total(zh)

    def b4(w, g):
        j = w * KVH + g
        take(w, g, B3, ROWS)
        result(w, g, fin[j] + r3[j].astype(F32))

    def w1(w, g):
        j = w * KVH + g
        for s in range(4):
            w0s[j, s] = pf[w, g, half(s, 1 - zh), :].astype(BF16)
        go(w, g, W0)

    def w2(w, g):
        j = w * KVH + g
        take(w, g, W0, 4 * ROWS)
        for s in range(4):
            pf[w, g, half(s, zh), :] += w0r[j, s].astype(F32)
        w1s[j, 0] = pf[w, g, quarter(yo, zh, 0), :].astype(BF16)
        w1s[j, 1] = pf[w, g, quarter(yo, zh, 1), :].astype(BF16)
        go(w, g, W1P, W1M)

    def w3(w, g):
        j = w * KVH + g
        w2s[j, 0, 64:, :] = pf[w, g, quarter(yp, zh, 1), :].astype(BF16)
        w2s[j, 1, :64, :] = pf[w, g, quarter(ym, zh, 0), :].astype(BF16)
        take(w, g, W1P, ROWS)
        w2s[j, 0, :64, :] = (pf[w, g, quarter(yp, zh, 0), :] + w1r[j, 0].astype(F32)).astype(BF16)
        go(w, g, W2P)
        w2s[j, 1, 64:, :] = (pf[w, g, quarter(ym, zh, 1), :] + w1r[j, 1].astype(F32)).astype(BF16)
        go(w, g, W2M)

    def w4(w, g):
        j = w * KVH + g
        take(w, g, W2P, 2 * ROWS)
        result(w, g, pf[w, g, own, :] + w2r[j, 0].astype(F32) + w2r[j, 1].astype(F32))

    def result(w, g, total):
        total = total.astype(BF16)
        if w:
            dk_ref[0, :, rng(g * HD, HD)] = total
        else:
            dv_ref[0, :, rng(g * HD, HD)] = total
            vgb[g // 2, rng(me * ROWS, ROWS), rng(lax.rem(g, 2) * HD, HD)] = total

    dv = [None] + [either(0, *two) for two in ((b1, w1), (b2, w2), (b3, w3), (b4, w4))]
    dk = [None] + [either(1, *two) for two in ((b1, w1), (b2, w2), (b3, w3), (b4, w4))]

    def send_h(k, z):
        xx, cc, to = near(k)
        return pltpu.make_async_remote_copy(
            src_ref=ht.at[rng(((xx * 2 + z) * 2 + cc) * 320, 320)],
            dst_ref=hg.at[z, :, rng(me * ROWS, ROWS)],
            send_sem=hs.at[0], recv_sem=hr.at[0], device_id=to, device_id_type=MESH,
        )

    def turn(i):
        dx, z = i // 2, lax.rem(i, 2)
        j = lax.rem(x + dx, 4) * 2 + z
        for n in range(5):
            at = j * 640 + n * 128
            ht[rng(at, 128), :] = hid[:, rng(at, 128)].T
        send_h(dx * 2 + 1, z).start()

        @pl.when(dx > 0)
        def _():
            send_h(dx * 2, z).start()

        @pl.when(dx == 0)
        def _():
            hg[z, :, rng(me * ROWS, ROWS)] = ht[rng((j * 2 + core) * 320, 320), :]

    def send_v(k, p, n, sem):
        rows = rng((lax.rem(x + n, 4) * 2 + core) * ROWS, ROWS)
        return pltpu.make_async_remote_copy(
            src_ref=vgb.at[p, rows], dst_ref=vgb.at[p, rows], send_sem=vs.at[0], recv_sem=sem.at[p],
            device_id=near(k)[2], device_id_type=MESH,
        )

    def send_w(k, p):
        t, to = along_z(k)
        return pltpu.make_async_remote_copy(
            src_ref=dws.at[p, t], dst_ref=dwr.at[p, k], send_sem=ws.at[0], recv_sem=wr.at[p],
            device_id=to, device_id_type=MESH,
        )

    def send_u(k, p):
        yy, to = along_y(k)
        return pltpu.make_async_remote_copy(
            src_ref=dus.at[p, yy], dst_ref=dur.at[p, k], send_sem=us.at[0], recv_sem=ur.at[p],
            device_id=to, device_id_type=MESH,
        )

    def weights1(p):
        each(1, 4, lambda n: send_v(2 * n, p, 0, vr).start())
        send_v(1, p, 0, vc).start()

    def weights1b(p):
        wait(vgb.at[p, pl.ds(0, 3 * ROWS)], vr.at[p])
        each(1, 4, lambda n: send_v(1, p, n, vc).start())

    def weights2(p):
        @pl.when(p == 0)
        def _():
            wait(hg.at[:, :, pl.ds(0, 7 * ROWS)], hr.at[0])

        wait(vgb.at[p, pl.ds(0, 4 * ROWS)], vc.at[p])
        res = dot(hg[...].reshape(640, SEQ), vgb[p], 1, 0).reshape(16, 40, 256)
        res = jnp.concatenate([res[:, :, :128], res[:, :, 128:]], axis=1).astype(BF16)
        for t in range(16):
            dws[p, t // 8 * 2 + t % 2, (t // 2) % 4] = res[t]
        each(1, 4, lambda k: send_w(k, p).start())

    def weights3(p):
        wait(dwr.at[p, pl.ds(0, 3)], wr.at[p])
        acc = dws[p, mine].astype(F32)
        for k in range(1, 4):
            acc = acc + dwr[p, k].astype(F32)
        dus[p] = acc.astype(BF16)
        each(1, 4, lambda k: send_u(k, p).start())

    def weights4(p):
        wait(dur.at[p, pl.ds(0, 3)], ur.at[p])
        acc = dus[p, y].astype(F32)
        for k in range(1, 4):
            acc = acc + dur[p, k].astype(F32)
        dw_ref[:, rng(p * 256, 128)] = acc[:40]
        dw_ref[:, rng(p * 256 + 128, 128)] = acc[40:]

    def at(i, when, count, f):
        lo, stride = when
        n = i - lo

        @pl.when((n >= 0) & (n < count * stride) & (lax.rem(n, stride) == 0))
        def _():
            f(n // stride)

    def first(g):
        rows_of(g)
        keys[3](g)
        pass1(g)
        dv[1](g)

    def second(g):
        values[3](g)
        pass2(g)

    def step(i, c):
        at(i, E4, KVH, dk[4])
        at(i, E3, KVH, dk[3])
        at(i, E2, KVH, dk[2])
        at(i, D4, KVH, dv[4])
        at(i, G1, 4, weights1)
        at(i, GB, 4, weights1b)
        at(i, G2, 4, weights2)
        at(i, G3, 4, weights3)
        at(i, G4, 4, weights4)
        at(i, D3, KVH, dv[3])
        at(i, D2, KVH, dv[2])
        at(i, K1, KVH, keys[1])
        at(i, K2, KVH, keys[2])
        at(i, V0, KVH, values[0])
        at(i, V1, KVH, values[1])
        at(i, V2, KVH, values[2])
        at(i, (0, 1), KVH, turn)
        at(i, P1, KVH, first)
        at(i, P2, KVH, second)
        return c

    lax.fori_loop(0, TICKS, step, 0)

    every = kvb.at[:, 0, pl.ds(0, SENT)]
    for w in range(2):
        for n in range(2):
            wait(every, send.at[w, n])
    wait(ob, dqsem.at[0])
    wait(hg.at[:, :, pl.ds(0, 7 * ROWS)], hs.at[0])
    wait(vgb.at[:, pl.ds(0, 7 * ROWS)], vs.at[0])
    wait(dws.at[:, pl.ds(0, 3)], ws.at[0])
    wait(dus.at[:, pl.ds(0, 3)], us.at[0])


def copy_out(dq, dk, dv, dw, dq_out, dk_out, dv_out, dw_out, dq_v, dk_v, dv_v, dw_v, into, out):
    parts = [(dk, dk_v, dk_out), (dv, dv_v, dv_out), (dw, dw_v, dw_out)]
    for n in range(8):
        cols = pl.ds(n * 1024, 1024)
        parts.append((dq.at[:, :, cols], dq_v.at[n], dq_out.at[:, :, cols]))
    reads = [pltpu.make_async_copy(a, b, into.at[n]) for n, (a, b, _) in enumerate(parts)]
    writes = [pltpu.make_async_copy(b, c, out.at[n]) for n, (_, b, c) in enumerate(parts)]
    for copy in reads:
        copy.start()
    for read, write in zip(reads, writes):
        read.wait()
        write.start()
    for copy in writes:
        copy.wait()


def body(hidden, q, k, v, o, do, lse, docs, order):
    anyspace = pl.BlockSpec(memory_space=pl.ANY)
    vmem = pl.BlockSpec(memory_space=pltpu.VMEM)
    smem = pl.BlockSpec(memory_space=pltpu.SMEM)
    dma = pltpu.SemaphoreType.DMA
    shapes = (
        jax.ShapeDtypeStruct((1, ROWS, KVH * GRP * HD), BF16),
        jax.ShapeDtypeStruct((1, ROWS, KVH * HD), BF16),
        jax.ShapeDtypeStruct((1, ROWS, KVH * HD), BF16),
        jax.ShapeDtypeStruct((40, KVH * HD), F32),
    )
    results = pl.pallas_call(
        kernel,
        out_shape=shapes,
        in_specs=[smem, smem] + [anyspace] * 7,
        out_specs=(anyspace, vmem, vmem, vmem),
        scratch_shapes=[
            pltpu.VMEM((KVH, 2, SEQ, HD), BF16),
            pltpu.VMEM((KVH, ROWS, GRP * HD), BF16),
            pltpu.VMEM((KVH, ROWS, GRP * HD), BF16),
            pltpu.VMEM((KVH, ROWS, GRP * HD), BF16),
            pltpu.VMEM((SEQ, ROWS), F32),
            pltpu.VMEM((KVH, 1, GRP * ROWS), F32),
            pltpu.VMEM((KVH, 1, GRP * ROWS), F32),
            pltpu.VMEM((2, KVH, SEQ, HD), F32),
            pltpu.VMEM((HD, GRP * ROWS), F32),
            pltpu.VMEM((KVH * GRP, ROWS), F32),
            pltpu.VMEM((2 * KVH, 2, ROWS, HD), BF16),
            pltpu.VMEM((2 * KVH, 2, ROWS, HD), BF16),
            pltpu.VMEM((2 * KVH, 2, 2 * ROWS, HD), BF16),
            pltpu.VMEM((2 * KVH, 2, 2 * ROWS, HD), BF16),
            pltpu.VMEM((2 * KVH, ROWS, HD), BF16),
            pltpu.VMEM((2 * KVH, ROWS, HD), BF16),
            pltpu.VMEM((2 * KVH, ROWS, HD), F32),
            pltpu.VMEM((2 * KVH, 4, ROWS, HD), BF16),
            pltpu.VMEM((2 * KVH, 4, ROWS, HD), BF16),
            pltpu.VMEM((2 * KVH, 2, 64, HD), BF16),
            pltpu.VMEM((2 * KVH, 2, 64, HD), BF16),
            pltpu.VMEM((2 * KVH, 2, ROWS, HD), BF16),
            pltpu.VMEM((2 * KVH, 2, ROWS, HD), BF16),
            pltpu.VMEM((ROWS, 5120), BF16),
            pltpu.VMEM((5120, ROWS), BF16),
            pltpu.VMEM((2, 320, SEQ), BF16),
            pltpu.VMEM((4, SEQ, 256), BF16),
            pltpu.VMEM((4, 4, 4, 80, 128), BF16),
            pltpu.VMEM((4, 4, 4, 80, 128), BF16),
            pltpu.VMEM((4, 4, 80, 128), BF16),
            pltpu.VMEM((4, 4, 80, 128), BF16),
            dma((2, 2)), dma((6, 2 * KVH)), dma((3,)), dma((KVH,)), dma((1,)),
            dma((1,)), dma((1,)), dma((1,)), dma((4,)), dma((4,)), dma((1,)), dma((4,)), dma((1,)), dma((4,)),
        ],
        compiler_params=pltpu.CompilerParams(
            collective_id=0, has_side_effects=True, vmem_limit_bytes=62 * 2**20
        ),
        name="attention_and_weights",
    )(docs, order, q, k, v, o, do, lse, hidden)
    return pl.pallas_call(
        copy_out,
        out_shape=shapes,
        in_specs=[anyspace] * 4,
        out_specs=(anyspace,) * 4,
        scratch_shapes=[
            pltpu.VMEM((8, 1, ROWS, 1024), BF16),
            pltpu.VMEM((1, ROWS, KVH * HD), BF16),
            pltpu.VMEM((1, ROWS, KVH * HD), BF16),
            pltpu.VMEM((40, KVH * HD), F32),
            dma((11,)), dma((11,)),
        ],
        name="copy_out",
    )(*results)


def solution(mesh):
    placed = (P("dp", "ctx", None),) * 6 + (P("dp", None, "ctx"), P("dp", None), P("dp", None))
    return jax.shard_map(
        body,
        mesh=mesh,
        in_specs=placed,
        out_specs=(P("dp", "ctx", None),) * 3 + (P(("dp", "ctx"), None),),
        check_vma=False,
    )
```
